32 devices in a mesh: tm: 8 (over z, x), chan: 4 (over y, core).
Axes of the slice: x: 2, y: 2, z: 4, core: 2. Of those that a mesh axis runs over, the one named last changes fastest.
Arguments:
- visibilities: bfloat16 [8, 8, 128, 512], P('tm', None, None, 'chan'), may hold values from -6 to 6
- station_gains: float32 [8, 192, 512], P(None, 'chan'), may hold values from -1.5 to 1.5, as said below
- station_pairs: int32 [128, 2], replicated, may hold values from 0 to 191, as said below
- average_bands: int32 [128, 2], replicated, may hold values from 0 to 3, as said below
- tile_map: int32 [128, 8], replicated, may hold values from 0 to 63
- baseline_order: int32 [128], replicated, may hold values from 0 to 127, as said below
Outputs:
- averaged: bfloat16 [8, 8, 128, 512], P(None, None, 'tm', 'chan')
- gridded: float32 [64, 8, 512], P('tm', None, 'chan')
The draws below stay inside these ranges and needn't reach their ends.
Inputs may be any that keep to these rules, and one draw needn't show every extreme that they name: `station_pairs`: row b holds the two stations of baseline b, the first smaller than the second. `average_bands`: column 0 is at most 3, column 1 at most 2. In each aligned block of 16 positions k of baseline_order, the bands of the baselines baseline_order[k] are, in some order, the pairs (3 - j % (3 + 1), 2 - j % (2 + 1)) for j = 0 to 15. `baseline_order`: each baseline once. `station_gains`: diagonal Jones entries have magnitudes of order one.
All inputs are finite; a program needn't handle non-finite values.
Results may differ from the reference program's by a relative error of at most 0.019.
Values may be sent and summed in bfloat16 or wider, within the bound.
A program may use at most 128 MiB of HBM per device.

```python
import math
import jax
import jax.numpy as jnp
from jax import lax

NS = 192
B_DEV = 16
TLOG = 3
CLOG = 2
NT = 8
NB = 128
NC = 512
TILES = 64


def draw_station_gains(key, part):
    streams = jax.random.split(key, 3)
    extent = (NS, NC)
    amplitude = jax.random.uniform(streams[0], (2,) + extent, jnp.float32, 0.5, 1.5)
    leakage = jnp.clip(0.2 * jax.random.normal(streams[2], (4,) + extent, jnp.float32), -0.6, 0.6)
    phase = jax.random.uniform(streams[1], (2,) + extent, jnp.float32, -math.pi, math.pi)
    real_part = amplitude * jnp.cos(phase)
    imag_part = amplitude * jnp.sin(phase)
    return jnp.stack([real_part[0], imag_part[0], leakage[0], leakage[1], leakage[2], leakage[3], real_part[1], imag_part[1]]).astype(jnp.float32)


def draw_station_pairs(key, part):
    streams = jax.random.split(key, 2)
    first = jax.random.randint(streams[0], (NB,), 0, NS)
    offset = jax.random.randint(streams[1], (NB,), 1, NS)
    second = (first + offset) % NS
    result = jnp.stack([jnp.minimum(first, second), jnp.maximum(first, second)], axis=1)
    result = result.at[0].set(jnp.array([0, NS - 1], jnp.int32))
    return result.astype(jnp.int32)


def band_layout(key):
    base = jax.random.fold_in(key, 4099)
    streams = jax.random.split(base, 2)
    order = jax.random.permutation(streams[0], NB).astype(jnp.int32)
    block_keys = jax.random.split(streams[1], NB // B_DEV)
    slots = jax.vmap(lambda single: jax.random.permutation(single, B_DEV))(block_keys).reshape(-1).astype(jnp.int32)
    time_levels = TLOG - slots % (TLOG + 1)
    chan_levels = CLOG - slots % (CLOG + 1)
    at_position = jnp.stack([time_levels, chan_levels], axis=1).astype(jnp.int32)
    bands = jnp.zeros((NB, 2), jnp.int32).at[order].set(at_position)
    return (order, bands)


def draw_average_bands(key, part):
    order, bands = band_layout(key)
    return bands.astype(jnp.int32)


def draw_baseline_order(key, part):
    order, bands = band_layout(key)
    return order.astype(jnp.int32)


def set_ends(drawn, key, least, high):
    spot = [jax.random.randint(jax.random.fold_in(key, axis), (), 0, length) for axis, length in enumerate(drawn.shape)]
    longest = drawn.shape.index(max(drawn.shape))
    beside = spot[:longest] + [(spot[longest] + 1) % drawn.shape[longest]] + spot[longest + 1:]
    return drawn.at[tuple(spot)].set(least).at[tuple(beside)].set(high)


def levels(key, shape, shards, smallest, top_value):
    level = 1.0
    for axis_at, blocks in shards:
        heights = jax.random.uniform(jax.random.fold_in(jax.random.fold_in(key, 6), axis_at), (blocks,), jnp.float32, smallest / len(shards), top_value / len(shards))
        level = level * jnp.repeat(jnp.exp(heights), shape[axis_at] // blocks).reshape((-1,) + (1,) * (len(shape) - 1 - axis_at))
    return level


def gaussian(stream_key, shape, scale, most, pieces=(), kind=jnp.bfloat16):
    gain = levels(stream_key, shape, pieces, -0.22, 0.18) if pieces else 1.0
    drawn = jax.random.normal(stream_key, shape, jnp.float32) * scale * gain
    return jnp.minimum(jnp.maximum(drawn, -most), most).astype(kind)


def setup_inputs(seed: int = 0) -> dict:
    splits = jax.random.split(jax.random.key(seed), 7)
    visibilities = gaussian(splits[0], (NT, 8, NB, NC), 1.0, 6.0, ((0, 8), (3, 4)))
    station_gains = draw_station_gains(jax.random.fold_in(splits[6], 71), 0)
    station_pairs = draw_station_pairs(jax.random.fold_in(splits[6], 71), 0)
    average_bands = draw_average_bands(jax.random.fold_in(splits[6], 71), 0)
    tile_map = set_ends(jax.random.randint(splits[4], (NB, NT), 0, TILES), jax.random.fold_in(splits[4], 1), 0, TILES - 1).astype(jnp.int32)
    baseline_order = draw_baseline_order(jax.random.fold_in(splits[6], 71), 0)
    return {"visibilities": visibilities, "station_gains": station_gains, "station_pairs": station_pairs, "average_bands": average_bands, "tile_map": tile_map, "baseline_order": baseline_order}


def product(left, right):
    return (left[0] * right[0] - left[1] * right[1], left[0] * right[1] + left[1] * right[0])


def product_conj(left, right):
    return (left[0] * right[0] + left[1] * right[1], left[1] * right[0] - left[0] * right[1])


def add_pair(left, right):
    return (left[0] + right[0], left[1] + right[1])


def as_matrix(components):
    return [[(components[0], components[1]), (components[2], components[3])],
            [(components[4], components[5]), (components[6], components[7])]]


def jones_apply(first, middle, second):
    left_gain = as_matrix(first)
    coherency = as_matrix(middle)
    right_gain = as_matrix(second)
    partial_rows = [[add_pair(product(left_gain[i][0], coherency[0][k]), product(left_gain[i][1], coherency[1][k])) for k in range(2)] for i in range(2)]
    result = []
    for i in range(2):
        for c in range(2):
            element = add_pair(product_conj(partial_rows[i][0], right_gain[c][0]), product_conj(partial_rows[i][1], right_gain[c][1]))
            result.extend(element)
    return result


def calibrate(samples, gain_table, first_station, second_station):
    left_gain = jnp.take(gain_table, first_station, axis=1)
    right_gain = jnp.take(gain_table, second_station, axis=1)
    values = [samples[:, i].astype(jnp.float32) for i in range(8)]
    result = jones_apply([left_gain[i][None] for i in range(8)], values, [right_gain[i][None] for i in range(8)])
    return jnp.stack(result, axis=1).astype(jnp.bfloat16)


def halve_time(current, size):
    extent = current.shape[0]
    shaped = current.reshape((extent // size, 2, size // 2) + current.shape[1:])
    merged = 0.5 * (shaped[:, 0:1] + shaped[:, 1:2])
    return jnp.broadcast_to(merged, shaped.shape).reshape(current.shape)


def halve_chan(current, size):
    extent = current.shape[-1]
    shaped = current.reshape(current.shape[:-1] + (extent // size, 2, size // 2))
    merged = 0.5 * (shaped[..., 0:1, :] + shaped[..., 1:2, :])
    return jnp.broadcast_to(merged, shaped.shape).reshape(current.shape)


def band_average(samples, time_levels, chan_levels):
    values = samples.astype(jnp.float32)
    time_select = time_levels[None, None, :, None]
    chan_select = chan_levels[None, None, :, None]
    result = values
    current = values
    for k in range(1, TLOG + 1):
        current = halve_time(current, 2 ** k)
        result = jnp.where(time_select >= k, current, result)
    final = result
    current = result
    for k in range(1, CLOG + 1):
        current = halve_chan(current, 2 ** k)
        final = jnp.where(chan_select >= k, current, final)
    return final.astype(jnp.bfloat16)


def reference(visibilities, station_gains, station_pairs, average_bands, tile_map, baseline_order):
    block_count = NB // B_DEV

    def advance(uv_grid, block):
        rows_here = lax.dynamic_slice_in_dim(baseline_order, block * B_DEV, B_DEV)
        samples = jnp.take(visibilities, rows_here, axis=2)
        pairs_here = station_pairs[rows_here]
        calibrated = calibrate(samples, station_gains, pairs_here[:, 0], pairs_here[:, 1])
        bands_here = average_bands[rows_here]
        averaged = band_average(calibrated, bands_here[:, 0], bands_here[:, 1])
        tile_here = tile_map[rows_here].T
        time_index = jnp.arange(NT, dtype=jnp.int32)[:, None]
        period = jnp.left_shift(jnp.ones_like(bands_here[:, 0]), bands_here[:, 0])[None, :]
        segment = jnp.where(time_index % period == 0, tile_here, TILES)
        values = jnp.transpose(averaged.astype(jnp.float32), (0, 2, 1, 3)).reshape(NT * B_DEV, 8, NC)
        summed = jax.ops.segment_sum(values, segment.reshape(-1), num_segments=TILES + 1)
        return uv_grid + summed[:TILES], averaged

    gridded, blocks = lax.scan(advance, jnp.zeros((TILES, 8, NC), jnp.float32), jnp.arange(block_count, dtype=jnp.int32))
    averaged = jnp.moveaxis(blocks, 0, 2).reshape(NT, 8, NB, NC)
    return averaged, gridded
```

```python
import functools

import jax
import jax.numpy as jnp
from jax import lax
from jax.experimental import pallas as pl
from jax.experimental.pallas import tpu as pltpu
from jax.sharding import PartitionSpec as P

TLOG = 3
CLOG = 2
LANES = 128
MESH = pl.DeviceIdType.MESH
F32 = jnp.float32
BF16 = jnp.bfloat16

ORDER, FIRST, SECOND, TBAND, CBAND, TILE0 = range(6)


def product(left, right):
    return (left[0] * right[0] - left[1] * right[1], left[0] * right[1] + left[1] * right[0])


def product_conj(left, right):
    return (left[0] * right[0] + left[1] * right[1], left[1] * right[0] - left[0] * right[1])


def add_pair(left, right):
    return (left[0] + right[0], left[1] + right[1])


def as_matrix(components):
    return [
        [(components[0], components[1]), (components[2], components[3])],
        [(components[4], components[5]), (components[6], components[7])],
    ]


def jones_apply(first, middle, second):
    left_gain = as_matrix(first)
    coherency = as_matrix(middle)
    right_gain = as_matrix(second)
    partial_rows = [
        [
            add_pair(
                product(left_gain[i][0], coherency[0][k]), product(left_gain[i][1], coherency[1][k])
            )
            for k in range(2)
        ]
        for i in range(2)
    ]
    result = []
    for i in range(2):
        for c in range(2):
            element = add_pair(
                product_conj(partial_rows[i][0], right_gain[c][0]),
                product_conj(partial_rows[i][1], right_gain[c][1]),
            )
            result.extend(element)
    return result


def split(values, width):
    return [values[:, i * width : (i + 1) * width] for i in range(8)]


def iota(shape, axis):
    return lax.broadcasted_iota(jnp.int32, shape, axis)


def dot(left, right):
    return jnp.dot(left, right, preferred_element_type=F32)


def one_hot(column, ids):
    return jnp.where(column == ids, 1.0, 0.0).astype(BF16)


def channel_means(width):
    row = iota((width, width), 0)
    column = iota((width, width), 1)
    means = []
    for level in range(1, CLOG + 1):
        same = (row >> level) == (column >> level)
        means.append(jnp.where(same, 2.0**-level, 0.0))
    return jnp.concatenate(means, axis=1).astype(BF16)


def channel_average(samples, means, level, width):
    averaged = dot(samples, means)
    result = samples.astype(F32)
    for k in range(1, CLOG + 1):
        result = jnp.where(level >= k, averaged[:, (k - 1) * width : k * width], result)
    return result


def kernel(
    n_tm, n_chan, vis_ref, gain_ref, index_ref, avg_ref, grid_ref,
    send, turned, gain_send, gains, table, chosen, calibrated, tiles_send, tiles,
    turn_out, turn_in, gain_out, gain_in, tile_out, tile_in,
):
    me = lax.axis_index("tm")
    mine = lax.axis_index("chan")
    baselines = vis_ref.shape[2]
    width = vis_ref.shape[3]
    rows = baselines // n_tm
    stations = gain_ref.shape[1]
    padded = gain_send.shape[1]
    tile_rows = grid_ref.shape[0]
    n_tiles = tile_rows * n_tm

    barrier = pltpu.get_barrier_semaphore()
    for step in range(1, n_tm):
        pl.semaphore_signal(
            barrier, inc=1, device_id={"tm": lax.rem(me + step, n_tm)}, device_id_type=MESH
        )
    for step in range(1, n_chan):
        pl.semaphore_signal(
            barrier, inc=1, device_id={"chan": lax.rem(mine + step, n_chan)}, device_id_type=MESH
        )

    index = index_ref[...]
    place = one_hot(index[:, ORDER : ORDER + 1], iota((baselines, baselines), 1))
    raw = jnp.concatenate([vis_ref[0, i] for i in range(8)], axis=1)
    send[...] = dot(place, raw).astype(BF16).reshape(send.shape)
    for c in range(n_chan):
        block = jnp.concatenate(
            [gain_ref[i, :, c * width : (c + 1) * width] for i in range(8)], axis=1
        )
        if padded > stations:
            block = jnp.concatenate(
                [block, jnp.zeros((padded - stations, 8 * width), F32)], axis=0
            )
        gain_send[c] = block.astype(BF16)

    pl.semaphore_wait(barrier, n_tm + n_chan - 2)

    copies = []
    gain_copies = []
    for step in range(1, n_chan):
        other = lax.rem(mine + step, n_chan)
        copy = pltpu.make_async_remote_copy(
            src_ref=gain_send.at[other],
            dst_ref=gains.at[mine],
            send_sem=gain_out.at[other],
            recv_sem=gain_in.at[mine],
            device_id={"chan": other},
            device_id_type=MESH,
        )
        copy.start()
        copies.append(copy)
    for step in range(1, n_tm):
        other = lax.rem(me + step, n_tm)
        copy = pltpu.make_async_remote_copy(
            src_ref=send.at[other],
            dst_ref=turned.at[me],
            send_sem=turn_out.at[other],
            recv_sem=turn_in.at[me],
            device_id={"tm": other},
            device_id_type=MESH,
        )
        copy.start()
        copies.append(copy)

    turned[me] = send[me]
    gains[mine] = gain_send[mine]
    means = channel_means(width)
    table[...] = dot(place, index.astype(F32).astype(BF16))

    ids = iota((1, n_chan * padded), 1)
    if padded > stations:
        lane = ids
        for c in range(n_chan):
            inside = (lane >= c * padded) & (lane < c * padded + stations)
            ids = jnp.where(inside, lane - c * (padded - stations), ids)
            ids = jnp.where((lane >= c * padded + stations) & (lane < (c + 1) * padded), -1, ids)
    here = pl.ds(pl.multiple_of(me * rows, rows), rows)
    at_all = table[...].astype(jnp.int32)
    at_here = table[here, :].astype(jnp.int32)
    pick = jnp.concatenate(
        [
            one_hot(at_all[:, FIRST : FIRST + 1], ids),
            one_hot(at_all[:, SECOND : SECOND + 1], ids),
            one_hot(at_here[:, FIRST : FIRST + 1], ids),
            one_hot(at_here[:, SECOND : SECOND + 1], ids),
        ],
        axis=0,
    )
    period = jnp.left_shift(jnp.ones((baselines, 1), jnp.int32), at_all[:, TBAND : TBAND + 1])
    start = me - (me & (period - 1))
    lane = iota((baselines, LANES), 1)
    tile = jnp.sum(
        jnp.where(lane == start + TILE0, table[...], 0.0), axis=1, keepdims=True
    ).astype(jnp.int32)
    wide = max(n_tiles, LANES)
    share = jnp.where(
        tile == iota((baselines, wide), 1), 1.0 / period.astype(F32), 0.0
    )
    share = share.T[:n_tiles].astype(BF16)

    for step in range(1, n_chan):
        other = lax.rem(mine + step, n_chan)
        pltpu.make_async_remote_copy(
            src_ref=gain_send.at[other],
            dst_ref=gains.at[other],
            send_sem=gain_out.at[other],
            recv_sem=gain_in.at[other],
            device_id={"chan": other},
            device_id_type=MESH,
        ).wait_recv()
    chosen[...] = dot(pick, gains[...].reshape(n_chan * padded, 8 * width))

    def calibrate_block(k, carry):
        at = pl.ds(pl.multiple_of(k * rows, rows), rows)
        at_second = pl.ds(pl.multiple_of(baselines + k * rows, rows), rows)
        result = jones_apply(
            split(chosen[at, :], width),
            split(send[k].astype(F32), width),
            split(chosen[at_second, :], width),
        )
        calibrated[at, :] = jnp.concatenate(result, axis=1).astype(BF16)
        return carry

    lax.fori_loop(0, n_tm, calibrate_block, 0, unroll=2)
    level = at_all[:, CBAND : CBAND + 1]
    sums = []
    for i in range(8):
        part = channel_average(calibrated[:, i * width : (i + 1) * width], means, level, width)
        sums.append(dot(share, part.astype(BF16)).reshape(n_tm, tile_rows, width))
    tiles_send[...] = jnp.concatenate(sums, axis=1).astype(BF16)
    for step in range(1, n_tm):
        other = lax.rem(me + step, n_tm)
        copy = pltpu.make_async_remote_copy(
            src_ref=tiles_send.at[other],
            dst_ref=tiles.at[me],
            send_sem=tile_out.at[other],
            recv_sem=tile_in.at[me],
            device_id={"tm": other},
            device_id_type=MESH,
        )
        copy.start()
        copies.append(copy)
    tiles[me] = tiles_send[me]

    for step in range(1, n_tm):
        other = lax.rem(me + step, n_tm)
        pltpu.make_async_remote_copy(
            src_ref=send.at[other],
            dst_ref=turned.at[other],
            send_sem=turn_out.at[other],
            recv_sem=turn_in.at[other],
            device_id={"tm": other},
            device_id_type=MESH,
        ).wait_recv()
    left = split(chosen[2 * baselines : 2 * baselines + rows, :], width)
    right = split(chosen[2 * baselines + rows : 2 * baselines + 2 * rows, :], width)

    def calibrate_time(t, carry):
        result = jones_apply(left, split(turned[t].astype(F32), width), right)
        at = pl.ds(pl.multiple_of(t * rows, rows), rows)
        calibrated[at, :] = jnp.concatenate(result, axis=1).astype(BF16)
        return carry

    lax.fori_loop(0, n_tm, calibrate_time, 0, unroll=2)
    group = 2**TLOG
    time_level = jnp.broadcast_to(at_here[:, TBAND : TBAND + 1], (rows, width))
    chan_level = jnp.broadcast_to(at_here[:, CBAND : CBAND + 1], (rows, width))
    chan_level = jnp.concatenate([chan_level] * group, axis=0)
    for first in range(0, n_tm, group):
        at = slice(first * rows, (first + group) * rows)
        for i in range(8):
            part = channel_average(
                calibrated[at, i * width : (i + 1) * width], means, chan_level, width
            )
            current = [part[t * rows : (t + 1) * rows] for t in range(group)]
            result = list(current)
            for k in range(1, TLOG + 1):
                current = [
                    0.5 * (current[2 * j] + current[2 * j + 1]) for j in range(len(current) // 2)
                ]
                result = [
                    jnp.where(time_level >= k, current[t >> k], result[t]) for t in range(group)
                ]
            for t in range(group):
                avg_ref[first + t, i] = result[t].astype(BF16)

    for step in range(1, n_tm):
        other = lax.rem(me + step, n_tm)
        pltpu.make_async_remote_copy(
            src_ref=tiles_send.at[other],
            dst_ref=tiles.at[other],
            send_sem=tile_out.at[other],
            recv_sem=tile_in.at[other],
            device_id={"tm": other},
            device_id_type=MESH,
        ).wait_recv()
    total = tiles[0].astype(F32)
    for m in range(1, n_tm):
        total = total + tiles[m].astype(F32)
    for i in range(8):
        grid_ref[:, i, :] = total[i * tile_rows : (i + 1) * tile_rows]
    for copy in copies:
        copy.wait_send()


def shards(n_tm, n_chan, tile_count, visibilities, station_gains, station_pairs, average_bands, tile_map, baseline_order):
    baselines, width = visibilities.shape[2:]
    rows = baselines // n_tm
    stations = station_gains.shape[1]
    padded = -(-stations // 16) * 16
    tile_rows = tile_count // n_tm
    index = jnp.concatenate(
        [baseline_order[:, None], station_pairs, average_bands, tile_map], axis=1
    )
    index = jnp.pad(index, ((0, 0), (0, LANES - index.shape[1])))
    vmem = pl.BlockSpec(memory_space=pltpu.VMEM)
    dma = pltpu.SemaphoreType.DMA
    return pl.pallas_call(
        functools.partial(kernel, n_tm, n_chan),
        out_shape=(
            jax.ShapeDtypeStruct((n_tm, 8, rows, width), BF16),
            jax.ShapeDtypeStruct((tile_rows, 8, width), F32),
        ),
        in_specs=[vmem] * 3,
        out_specs=(vmem, vmem),
        scratch_shapes=[
            pltpu.VMEM((n_tm, rows, 8 * width), BF16),
            pltpu.VMEM((n_tm, rows, 8 * width), BF16),
            pltpu.VMEM((n_chan, padded, 8 * width), BF16),
            pltpu.VMEM((n_chan, padded, 8 * width), BF16),
            pltpu.VMEM((baselines, LANES), F32),
            pltpu.VMEM((2 * baselines + 2 * rows, 8 * width), F32),
            pltpu.VMEM((baselines, 8 * width), BF16),
            pltpu.VMEM((n_tm, 8 * tile_rows, width), BF16),
            pltpu.VMEM((n_tm, 8 * tile_rows, width), BF16),
            dma((n_tm,)),
            dma((n_tm,)),
            dma((n_chan,)),
            dma((n_chan,)),
            dma((n_tm,)),
            dma((n_tm,)),
        ],
        compiler_params=pltpu.CompilerParams(
            collective_id=0, has_side_effects=True, vmem_limit_bytes=40 * 2**20
        ),
        cost_estimate=pl.CostEstimate(
            flops=2 * 10**8, bytes_accessed=2 * 10**6, transcendentals=0
        ),
    )(visibilities, station_gains, index)


def solution(mesh):
    n_tm, n_chan = mesh.shape["tm"], mesh.shape["chan"]
    tile_count = 8 * n_tm
    return jax.shard_map(
        functools.partial(shards, n_tm, n_chan, tile_count),
        mesh=mesh,
        in_specs=(P("tm", None, None, "chan"), P(None, "chan", None), P(), P(), P(), P()),
        out_specs=(P(None, None, "tm", "chan"), P("tm", None, "chan")),
        check_vma=False,
    )
```

```python
import functools

import jax
import jax.numpy as jnp
from jax import lax
from jax.experimental import pallas as pl
from jax.experimental.pallas import tpu as pltpu
from jax.sharding import PartitionSpec as P

TLOG = 3
CLOG = 2
LANES = 128
MESH = pl.DeviceIdType.MESH
F32 = jnp.float32
BF16 = jnp.bfloat16


def product(left, right):
    return (left[0] * right[0] - left[1] * right[1], left[0] * right[1] + left[1] * right[0])


def product_conj(left, right):
    return (left[0] * right[0] + left[1] * right[1], left[1] * right[0] - left[0] * right[1])


def add_pair(left, right):
    return (left[0] + right[0], left[1] + right[1])


def as_matrix(components):
    return [
        [(components[0], components[1]), (components[2], components[3])],
        [(components[4], components[5]), (components[6], components[7])],
    ]


def jones_apply(first, middle, second):
    left_gain = as_matrix(first)
    coherency = as_matrix(middle)
    right_gain = as_matrix(second)
    partial_rows = [
        [
            add_pair(
                product(left_gain[i][0], coherency[0][k]), product(left_gain[i][1], coherency[1][k])
            )
            for k in range(2)
        ]
        for i in range(2)
    ]
    result = []
    for i in range(2):
        for c in range(2):
            element = add_pair(
                product_conj(partial_rows[i][0], right_gain[c][0]),
                product_conj(partial_rows[i][1], right_gain[c][1]),
            )
            result.extend(element)
    return result


def split(values, width):
    return [values[:, i * width : (i + 1) * width] for i in range(8)]


def iota(shape, axis):
    return lax.broadcasted_iota(jnp.int32, shape, axis)


def dot(left, right):
    return jnp.dot(left, right, preferred_element_type=F32)


def one_hot(column, ids):
    return jnp.where(column == ids, 1.0, 0.0).astype(BF16)


def channel_means(width):
    row = iota((width, width), 0)
    column = iota((width, width), 1)
    means = []
    for level in range(1, CLOG + 1):
        same = (row >> level) == (column >> level)
        means.append(jnp.where(same, 2.0**-level, 0.0))
    return jnp.concatenate(means, axis=1).astype(BF16)


def channel_average(samples, means, level, width):
    averaged = dot(samples, means)
    result = samples.astype(F32)
    for k in range(1, CLOG + 1):
        result = jnp.where(level >= k, averaged[:, (k - 1) * width : k * width], result)
    return result


def kernel(
    n_tm, n_chan,
    vis_hbm, gain_hbm, pairs_hbm, bands_hbm, map_hbm, order_hbm, avg_ref, grid_ref,
    vis_ref, gain_ref, pairs_ref, bands_ref, map_ref, order_ref, local, index,
    send, turned, gain_send, gains, table, chosen, calibrated, tiles_send, tiles,
    turn_out, turn_in, gain_out, gain_in, tile_out, tile_in,
):
    me = lax.axis_index("tm")
    mine = lax.axis_index("chan")
    baselines = vis_ref.shape[1]
    width = vis_ref.shape[2]
    rows = baselines // n_tm
    stations = gain_ref.shape[1]
    padded = gain_send.shape[1]
    tile_rows = grid_ref.shape[0]
    n_tiles = tile_rows * n_tm
    times = map_ref.shape[0]
    first_at, second_at, time_at, chan_at = range(times, times + 4)

    sources = (order_hbm, gain_hbm, vis_hbm.at[0], pairs_hbm, bands_hbm, map_hbm)
    targets = (order_ref, gain_ref, vis_ref, pairs_ref, bands_ref, map_ref)
    loads = [
        pltpu.make_async_copy(source, target, local.at[i])
        for i, (source, target) in enumerate(zip(sources, targets))
    ]
    for load in loads:
        load.start()

    barrier = pltpu.get_barrier_semaphore()
    for step in range(1, n_tm):
        pl.semaphore_signal(
            barrier, inc=1, device_id={"tm": lax.rem(me + step, n_tm)}, device_id_type=MESH
        )
    for step in range(1, n_chan):
        pl.semaphore_signal(
            barrier, inc=1, device_id={"chan": lax.rem(mine + step, n_chan)}, device_id_type=MESH
        )

    index[...] = jnp.zeros_like(index)
    loads[0].wait()
    place = jnp.where(order_ref[...] == iota((baselines, baselines), 0), 1.0, 0.0)
    loads[1].wait()
    for c in range(n_chan):
        block = jnp.concatenate(
            [gain_ref[i, :, c * width : (c + 1) * width] for i in range(8)], axis=1
        )
        if padded > stations:
            block = jnp.concatenate(
                [block, jnp.zeros((padded - stations, 8 * width), F32)], axis=0
            )
        gain_send[c] = block.astype(BF16)

    place = place.T.astype(BF16)
    loads[2].wait()
    raw = jnp.concatenate([vis_ref[i] for i in range(8)], axis=1)
    send[...] = dot(place, raw).astype(BF16).reshape(send.shape)

    pl.semaphore_wait(barrier, n_tm + n_chan - 2)

    copies = []
    gain_copies = []
    for step in range(1, n_chan):
        other = lax.rem(mine + step, n_chan)
        copy = pltpu.make_async_remote_copy(
            src_ref=gain_send.at[other],
            dst_ref=gains.at[mine],
            send_sem=gain_out.at[other],
            recv_sem=gain_in.at[mine],
            device_id={"chan": other},
            device_id_type=MESH,
        )
        copy.start()
        copies.append(copy)
    for step in range(1, n_tm):
        other = lax.rem(me + step, n_tm)
        copy = pltpu.make_async_remote_copy(
            src_ref=send.at[other],
            dst_ref=turned.at[me],
            send_sem=turn_out.at[other],
            recv_sem=turn_in.at[me],
            device_id={"tm": other},
            device_id_type=MESH,
        )
        copy.start()
        copies.append(copy)

    turned[me] = send[me]
    gains[mine] = gain_send[mine]
    means = channel_means(width)
    for load in loads[3:]:
        load.wait()
    index[:times] = map_ref[...].astype(F32)
    index[first_at : second_at + 1] = pairs_ref[...].astype(F32)
    index[time_at : chan_at + 1] = bands_ref[...].astype(F32)
    table[...] = lax.dot_general(
        place, index[...].astype(BF16), (((1,), (1,)), ((), ())), preferred_element_type=F32
    )

    ids = iota((1, n_chan * padded), 1)
    if padded > stations:
        lane = ids
        for c in range(n_chan):
            inside = (lane >= c * padded) & (lane < c * padded + stations)
            ids = jnp.where(inside, lane - c * (padded - stations), ids)
            ids = jnp.where((lane >= c * padded + stations) & (lane < (c + 1) * padded), -1, ids)
    here = pl.ds(pl.multiple_of(me * rows, rows), rows)
    at_all = table[...].astype(jnp.int32)
    at_here = table[here, :].astype(jnp.int32)
    pick = jnp.concatenate(
        [
            one_hot(at_all[:, first_at : first_at + 1], ids),
            one_hot(at_all[:, second_at : second_at + 1], ids),
            one_hot(at_here[:, first_at : first_at + 1], ids),
            one_hot(at_here[:, second_at : second_at + 1], ids),
        ],
        axis=0,
    )
    period = jnp.left_shift(jnp.ones((baselines, 1), jnp.int32), at_all[:, time_at : time_at + 1])
    start = me - (me & (period - 1))
    lane = iota((baselines, LANES), 1)
    tile = jnp.sum(
        jnp.where(lane == start, table[...], 0.0), axis=1, keepdims=True
    ).astype(jnp.int32)
    wide = max(n_tiles, LANES)
    share = jnp.where(
        tile == iota((baselines, wide), 1), 1.0 / period.astype(F32), 0.0
    )
    share = share.T[:n_tiles].astype(BF16)

    for step in range(1, n_chan):
        other = lax.rem(mine + step, n_chan)
        pltpu.make_async_remote_copy(
            src_ref=gain_send.at[other],
            dst_ref=gains.at[other],
            send_sem=gain_out.at[other],
            recv_sem=gain_in.at[other],
            device_id={"chan": other},
            device_id_type=MESH,
        ).wait_recv()
    chosen[...] = dot(pick, gains[...].reshape(n_chan * padded, 8 * width))

    def calibrate_block(k, carry):
        at = pl.ds(pl.multiple_of(k * rows, rows), rows)
        at_second = pl.ds(pl.multiple_of(baselines + k * rows, rows), rows)
        result = jones_apply(
            split(chosen[at, :], width),
            split(send[k].astype(F32), width),
            split(chosen[at_second, :], width),
        )
        calibrated[at, :] = jnp.concatenate(result, axis=1).astype(BF16)
        return carry

    lax.fori_loop(0, n_tm, calibrate_block, 0, unroll=2)
    level = at_all[:, chan_at : chan_at + 1]
    sums = []
    for i in range(8):
        part = channel_average(calibrated[:, i * width : (i + 1) * width], means, level, width)
        sums.append(dot(share, part.astype(BF16)).reshape(n_tm, tile_rows, width))
    tiles_send[...] = jnp.concatenate(sums, axis=1).astype(BF16)
    for step in range(1, n_tm):
        other = lax.rem(me + step, n_tm)
        copy = pltpu.make_async_remote_copy(
            src_ref=tiles_send.at[other],
            dst_ref=tiles.at[me],
            send_sem=tile_out.at[other],
            recv_sem=tile_in.at[me],
            device_id={"tm": other},
            device_id_type=MESH,
        )
        copy.start()
        copies.append(copy)
    tiles[me] = tiles_send[me]

    for step in range(1, n_tm):
        other = lax.rem(me + step, n_tm)
        pltpu.make_async_remote_copy(
            src_ref=send.at[other],
            dst_ref=turned.at[other],
            send_sem=turn_out.at[other],
            recv_sem=turn_in.at[other],
            device_id={"tm": other},
            device_id_type=MESH,
        ).wait_recv()
    left = split(chosen[2 * baselines : 2 * baselines + rows, :], width)
    right = split(chosen[2 * baselines + rows : 2 * baselines + 2 * rows, :], width)

    def calibrate_time(t, carry):
        result = jones_apply(left, split(turned[t].astype(F32), width), right)
        at = pl.ds(pl.multiple_of(t * rows, rows), rows)
        calibrated[at, :] = jnp.concatenate(result, axis=1).astype(BF16)
        return carry

    lax.fori_loop(0, n_tm, calibrate_time, 0, unroll=2)
    group = 2**TLOG
    time_level = jnp.broadcast_to(at_here[:, time_at : time_at + 1], (rows, width))
    chan_level = jnp.broadcast_to(at_here[:, chan_at : chan_at + 1], (rows, width))
    chan_level = jnp.concatenate([chan_level] * group, axis=0)
    for first in range(0, n_tm, group):
        at = slice(first * rows, (first + group) * rows)
        for i in range(8):
            part = channel_average(
                calibrated[at, i * width : (i + 1) * width], means, chan_level, width
            )
            current = [part[t * rows : (t + 1) * rows] for t in range(group)]
            result = list(current)
            for k in range(1, TLOG + 1):
                current = [
                    0.5 * (current[2 * j] + current[2 * j + 1]) for j in range(len(current) // 2)
                ]
                result = [
                    jnp.where(time_level >= k, current[t >> k], result[t]) for t in range(group)
                ]
            for t in range(group):
                avg_ref[first + t, i] = result[t].astype(BF16)

    for step in range(1, n_tm):
        other = lax.rem(me + step, n_tm)
        pltpu.make_async_remote_copy(
            src_ref=tiles_send.at[other],
            dst_ref=tiles.at[other],
            send_sem=tile_out.at[other],
            recv_sem=tile_in.at[other],
            device_id={"tm": other},
            device_id_type=MESH,
        ).wait_recv()
    total = tiles[0].astype(F32)
    for m in range(1, n_tm):
        total = total + tiles[m].astype(F32)
    for i in range(8):
        grid_ref[:, i, :] = total[i * tile_rows : (i + 1) * tile_rows]
    for copy in copies:
        copy.wait_send()


def shards(n_tm, n_chan, tile_count, visibilities, station_gains, station_pairs, average_bands, tile_map, baseline_order):
    baselines, width = visibilities.shape[2:]
    rows = baselines // n_tm
    stations = station_gains.shape[1]
    padded = -(-stations // 16) * 16
    tile_rows = tile_count // n_tm
    vmem = pl.BlockSpec(memory_space=pltpu.VMEM)
    dma = pltpu.SemaphoreType.DMA
    hbm = functools.partial(pltpu.with_memory_space_constraint, memory_space=pltpu.HBM)
    return pl.pallas_call(
        functools.partial(kernel, n_tm, n_chan),
        out_shape=(
            pltpu.VMEM((n_tm, 8, rows, width), BF16),
            pltpu.VMEM((tile_rows, 8, width), F32),
        ),
        in_specs=[pl.BlockSpec(memory_space=pl.ANY)] * 6,
        out_specs=(vmem, vmem),
        scratch_shapes=[
            pltpu.VMEM((8, baselines, width), BF16),
            pltpu.VMEM(station_gains.shape, F32),
            pltpu.VMEM((2, baselines), jnp.int32),
            pltpu.VMEM((2, baselines), jnp.int32),
            pltpu.VMEM((n_tm, baselines), jnp.int32),
            pltpu.VMEM((1, baselines), jnp.int32),
            dma((6,)),
            pltpu.VMEM((LANES, baselines), F32),
            pltpu.VMEM((n_tm, rows, 8 * width), BF16),
            pltpu.VMEM((n_tm, rows, 8 * width), BF16),
            pltpu.VMEM((n_chan, padded, 8 * width), BF16),
            pltpu.VMEM((n_chan, padded, 8 * width), BF16),
            pltpu.VMEM((baselines, LANES), F32),
            pltpu.VMEM((2 * baselines + 2 * rows, 8 * width), F32),
            pltpu.VMEM((baselines, 8 * width), BF16),
            pltpu.VMEM((n_tm, 8 * tile_rows, width), BF16),
            pltpu.VMEM((n_tm, 8 * tile_rows, width), BF16),
            dma((n_tm,)),
            dma((n_tm,)),
            dma((n_chan,)),
            dma((n_chan,)),
            dma((n_tm,)),
            dma((n_tm,)),
        ],
        compiler_params=pltpu.CompilerParams(
            collective_id=0, has_side_effects=True, vmem_limit_bytes=40 * 2**20
        ),
        cost_estimate=pl.CostEstimate(
            flops=2 * 10**8, bytes_accessed=2 * 10**6, transcendentals=0
        ),
    )(
        hbm(visibilities),
        hbm(station_gains),
        hbm(station_pairs.T),
        hbm(average_bands.T),
        hbm(tile_map.T),
        hbm(baseline_order.reshape(1, baselines)),
    )


def solution(mesh):
    n_tm, n_chan = mesh.shape["tm"], mesh.shape["chan"]
    tile_count = 8 * n_tm
    return jax.shard_map(
        functools.partial(shards, n_tm, n_chan, tile_count),
        mesh=mesh,
        in_specs=(P("tm", None, None, "chan"), P(None, "chan", None), P(), P(), P(), P()),
        out_specs=(P(None, None, "tm", "chan"), P("tm", None, "chan")),
        check_vma=False,
    )
```

```python
import functools

import jax
import jax.numpy as jnp
from jax import lax
from jax.experimental import pallas as pl
from jax.experimental.pallas import tpu as pltpu
from jax.sharding import PartitionSpec as P

TLOG = 3
CLOG = 2
LANES = 128
MESH = pl.DeviceIdType.MESH
F32 = jnp.float32
BF16 = jnp.bfloat16


def product(left, right):
    return (left[0] * right[0] - left[1] * right[1], left[0] * right[1] + left[1] * right[0])


def product_conj(left, right):
    return (left[0] * right[0] + left[1] * right[1], left[1] * right[0] - left[0] * right[1])


def add_pair(left, right):
    return (left[0] + right[0], left[1] + right[1])


def as_matrix(components):
    return [
        [(components[0], components[1]), (components[2], components[3])],
        [(components[4], components[5]), (components[6], components[7])],
    ]


def jones_apply(first, middle, second):
    left_gain = as_matrix(first)
    coherency = as_matrix(middle)
    right_gain = as_matrix(second)
    partial_rows = [
        [
            add_pair(
                product(left_gain[i][0], coherency[0][k]), product(left_gain[i][1], coherency[1][k])
            )
            for k in range(2)
        ]
        for i in range(2)
    ]
    result = []
    for i in range(2):
        for c in range(2):
            element = add_pair(
                product_conj(partial_rows[i][0], right_gain[c][0]),
                product_conj(partial_rows[i][1], right_gain[c][1]),
            )
            result.extend(element)
    return result


def split(values, width):
    return [values[:, i * width : (i + 1) * width] for i in range(8)]


def iota(shape, axis):
    return lax.broadcasted_iota(jnp.int32, shape, axis)


def dot(left, right):
    return jnp.dot(left, right, preferred_element_type=F32)


def one_hot(column, ids):
    return jnp.where(column == ids, 1.0, 0.0).astype(BF16)


def channel_means(width):
    row = iota((width, width), 0)
    column = iota((width, width), 1)
    means = []
    for level in range(1, CLOG + 1):
        same = (row >> level) == (column >> level)
        means.append(jnp.where(same, 2.0**-level, 0.0))
    return jnp.concatenate(means, axis=1).astype(BF16)


def channel_average(samples, means, level, width):
    averaged = dot(samples, means)
    result = samples.astype(F32)
    for k in range(1, CLOG + 1):
        result = jnp.where(level >= k, averaged[:, (k - 1) * width : k * width], result)
    return result


def kernel(
    n_tm, n_chan,
    vis_hbm, gain_hbm, pairs_hbm, bands_hbm, map_hbm, order_hbm, avg_ref, tiles_ref,
    vis_ref, gain_ref, pairs_ref, bands_ref, map_ref, order_ref, local, index,
    send, turned, gain_send, gains, table, chosen, calibrated, tiles_send, tiles,
    turn_out, turn_in, gain_out, gain_in, tile_out, tile_in,
):
    me = lax.axis_index("tm")
    mine = lax.axis_index("chan")
    baselines = vis_ref.shape[1]
    width = vis_ref.shape[2]
    rows = baselines // n_tm
    stations = gain_ref.shape[1]
    padded = gain_send.shape[1]
    tile_rows = tiles_ref.shape[1] // 8
    n_tiles = tile_rows * n_tm
    times = map_ref.shape[0]
    first_at, second_at, time_at, chan_at = range(times, times + 4)

    sources = (order_hbm, gain_hbm, vis_hbm.at[0], pairs_hbm, bands_hbm, map_hbm)
    targets = (order_ref, gain_ref, vis_ref, pairs_ref, bands_ref, map_ref)
    loads = [
        pltpu.make_async_copy(source, target, local.at[i])
        for i, (source, target) in enumerate(zip(sources, targets))
    ]
    for load in loads:
        load.start()

    barrier = pltpu.get_barrier_semaphore()
    for step in range(1, n_tm):
        pl.semaphore_signal(
            barrier, inc=1, device_id={"tm": lax.rem(me + step, n_tm)}, device_id_type=MESH
        )
    for step in range(1, n_chan):
        pl.semaphore_signal(
            barrier, inc=1, device_id={"chan": lax.rem(mine + step, n_chan)}, device_id_type=MESH
        )

    index[...] = jnp.zeros_like(index)
    loads[0].wait()
    place = jnp.where(order_ref[...] == iota((baselines, baselines), 0), 1.0, 0.0)
    loads[1].wait()
    for c in range(n_chan):
        block = jnp.concatenate(
            [gain_ref[i, :, c * width : (c + 1) * width] for i in range(8)], axis=1
        )
        if padded > stations:
            block = jnp.concatenate(
                [block, jnp.zeros((padded - stations, 8 * width), F32)], axis=0
            )
        gain_send[c] = block.astype(BF16)

    place = place.T.astype(BF16)
    loads[2].wait()
    raw = jnp.concatenate([vis_ref[i] for i in range(8)], axis=1)
    send[...] = dot(place, raw).astype(BF16).reshape(send.shape)

    pl.semaphore_wait(barrier, n_tm + n_chan - 2)

    copies = []
    gain_copies = []
    for step in range(1, n_chan):
        other = lax.rem(mine + step, n_chan)
        copy = pltpu.make_async_remote_copy(
            src_ref=gain_send.at[other],
            dst_ref=gains.at[mine],
            send_sem=gain_out.at[other],
            recv_sem=gain_in.at[mine],
            device_id={"chan": other},
            device_id_type=MESH,
        )
        copy.start()
        copies.append(copy)
    for step in range(1, n_tm):
        other = lax.rem(me + step, n_tm)
        copy = pltpu.make_async_remote_copy(
            src_ref=send.at[other],
            dst_ref=turned.at[me],
            send_sem=turn_out.at[other],
            recv_sem=turn_in.at[me],
            device_id={"tm": other},
            device_id_type=MESH,
        )
        copy.start()
        copies.append(copy)

    turned[me] = send[me]
    gains[mine] = gain_send[mine]
    means = channel_means(width)
    for load in loads[3:]:
        load.wait()
    index[:times] = map_ref[...].astype(F32)
    index[first_at : second_at + 1] = pairs_ref[...].astype(F32)
    index[time_at : chan_at + 1] = bands_ref[...].astype(F32)
    table[...] = lax.dot_general(
        place, index[...].astype(BF16), (((1,), (1,)), ((), ())), preferred_element_type=F32
    )

    ids = iota((1, n_chan * padded), 1)
    if padded > stations:
        lane = ids
        for c in range(n_chan):
            inside = (lane >= c * padded) & (lane < c * padded + stations)
            ids = jnp.where(inside, lane - c * (padded - stations), ids)
            ids = jnp.where((lane >= c * padded + stations) & (lane < (c + 1) * padded), -1, ids)
    here = pl.ds(pl.multiple_of(me * rows, rows), rows)
    at_all = table[...].astype(jnp.int32)
    at_here = table[here, :].astype(jnp.int32)
    pick = jnp.concatenate(
        [
            one_hot(at_all[:, first_at : first_at + 1], ids),
            one_hot(at_all[:, second_at : second_at + 1], ids),
            one_hot(at_here[:, first_at : first_at + 1], ids),
            one_hot(at_here[:, second_at : second_at + 1], ids),
        ],
        axis=0,
    )
    period = jnp.left_shift(jnp.ones((baselines, 1), jnp.int32), at_all[:, time_at : time_at + 1])
    start = me - (me & (period - 1))
    lane = iota((baselines, LANES), 1)
    tile = jnp.sum(
        jnp.where(lane == start, table[...], 0.0), axis=1, keepdims=True
    ).astype(jnp.int32)
    wide = max(n_tiles, LANES)
    share = jnp.where(
        tile == iota((baselines, wide), 1), 1.0 / period.astype(F32), 0.0
    )
    share = share.T[:n_tiles].astype(BF16)

    for step in range(1, n_chan):
        other = lax.rem(mine + step, n_chan)
        pltpu.make_async_remote_copy(
            src_ref=gain_send.at[other],
            dst_ref=gains.at[other],
            send_sem=gain_out.at[other],
            recv_sem=gain_in.at[other],
            device_id={"chan": other},
            device_id_type=MESH,
        ).wait_recv()
    chosen[...] = dot(pick, gains[...].reshape(n_chan * padded, 8 * width))

    def calibrate_block(k, carry):
        at = pl.ds(pl.multiple_of(k * rows, rows), rows)
        at_second = pl.ds(pl.multiple_of(baselines + k * rows, rows), rows)
        result = jones_apply(
            split(chosen[at, :], width),
            split(send[k].astype(F32), width),
            split(chosen[at_second, :], width),
        )
        calibrated[at, :] = jnp.concatenate(result, axis=1).astype(BF16)
        return carry

    lax.fori_loop(0, n_tm, calibrate_block, 0, unroll=2)
    level = at_all[:, chan_at : chan_at + 1]
    sums = []
    for i in range(8):
        part = channel_average(calibrated[:, i * width : (i + 1) * width], means, level, width)
        sums.append(dot(share, part.astype(BF16)).reshape(n_tm, tile_rows, width))
    tiles_send[...] = jnp.concatenate(sums, axis=1).astype(BF16)
    for step in range(1, n_tm):
        other = lax.rem(me + step, n_tm)
        copy = pltpu.make_async_remote_copy(
            src_ref=tiles_send.at[other],
            dst_ref=tiles.at[me],
            send_sem=tile_out.at[other],
            recv_sem=tile_in.at[me],
            device_id={"tm": other},
            device_id_type=MESH,
        )
        copy.start()
        copies.append(copy)
    tiles[me] = tiles_send[me]

    for step in range(1, n_tm):
        other = lax.rem(me + step, n_tm)
        pltpu.make_async_remote_copy(
            src_ref=send.at[other],
            dst_ref=turned.at[other],
            send_sem=turn_out.at[other],
            recv_sem=turn_in.at[other],
            device_id={"tm": other},
            device_id_type=MESH,
        ).wait_recv()
    left = split(chosen[2 * baselines : 2 * baselines + rows, :], width)
    right = split(chosen[2 * baselines + rows : 2 * baselines + 2 * rows, :], width)

    def calibrate_time(t, carry):
        result = jones_apply(left, split(turned[t].astype(F32), width), right)
        at = pl.ds(pl.multiple_of(t * rows, rows), rows)
        calibrated[at, :] = jnp.concatenate(result, axis=1).astype(BF16)
        return carry

    lax.fori_loop(0, n_tm, calibrate_time, 0, unroll=2)
    group = 2**TLOG
    time_level = jnp.broadcast_to(at_here[:, time_at : time_at + 1], (rows, width))
    chan_level = jnp.broadcast_to(at_here[:, chan_at : chan_at + 1], (rows, width))
    chan_level = jnp.concatenate([chan_level] * group, axis=0)
    for first in range(0, n_tm, group):
        at = slice(first * rows, (first + group) * rows)
        for i in range(8):
            part = channel_average(
                calibrated[at, i * width : (i + 1) * width], means, chan_level, width
            )
            current = [part[t * rows : (t + 1) * rows] for t in range(group)]
            result = list(current)
            for k in range(1, TLOG + 1):
                current = [
                    0.5 * (current[2 * j] + current[2 * j + 1]) for j in range(len(current) // 2)
                ]
                result = [
                    jnp.where(time_level >= k, current[t >> k], result[t]) for t in range(group)
                ]
            for t in range(group):
                avg_ref[first + t, i] = result[t].astype(BF16)

    for step in range(1, n_tm):
        other = lax.rem(me + step, n_tm)
        pltpu.make_async_remote_copy(
            src_ref=tiles_send.at[other],
            dst_ref=tiles.at[other],
            send_sem=tile_out.at[other],
            recv_sem=tile_in.at[other],
            device_id={"tm": other},
            device_id_type=MESH,
        ).wait_recv()
    tiles_ref[...] = tiles[...]
    for copy in copies:
        copy.wait_send()


def write_kernel(avg_ref, tiles_ref, avg_hbm, grid_hbm, grid, done):
    averaged = pltpu.make_async_copy(avg_ref, avg_hbm, done.at[0])
    averaged.start()
    tile_rows = grid.shape[0]
    total = tiles_ref[0].astype(F32)
    for m in range(1, tiles_ref.shape[0]):
        total = total + tiles_ref[m].astype(F32)
    for i in range(8):
        grid[:, i, :] = total[i * tile_rows : (i + 1) * tile_rows]
    gridded = pltpu.make_async_copy(grid, grid_hbm, done.at[1])
    gridded.start()
    averaged.wait()
    gridded.wait()


def shards(n_tm, n_chan, tile_count, visibilities, station_gains, station_pairs, average_bands, tile_map, baseline_order):
    baselines, width = visibilities.shape[2:]
    rows = baselines // n_tm
    stations = station_gains.shape[1]
    padded = -(-stations // 16) * 16
    tile_rows = tile_count // n_tm
    vmem = pl.BlockSpec(memory_space=pltpu.VMEM)
    dma = pltpu.SemaphoreType.DMA
    hbm = functools.partial(pltpu.with_memory_space_constraint, memory_space=pltpu.HBM)
    averaged, tiles = pl.pallas_call(
        functools.partial(kernel, n_tm, n_chan),
        out_shape=(
            pltpu.VMEM((n_tm, 8, rows, width), BF16),
            pltpu.VMEM((n_tm, 8 * tile_rows, width), BF16),
        ),
        in_specs=[pl.BlockSpec(memory_space=pl.ANY)] * 6,
        out_specs=(vmem, vmem),
        scratch_shapes=[
            pltpu.VMEM((8, baselines, width), BF16),
            pltpu.VMEM(station_gains.shape, F32),
            pltpu.VMEM((2, baselines), jnp.int32),
            pltpu.VMEM((2, baselines), jnp.int32),
            pltpu.VMEM((n_tm, baselines), jnp.int32),
            pltpu.VMEM((1, baselines), jnp.int32),
            dma((6,)),
            pltpu.VMEM((LANES, baselines), F32),
            pltpu.VMEM((n_tm, rows, 8 * width), BF16),
            pltpu.VMEM((n_tm, rows, 8 * width), BF16),
            pltpu.VMEM((n_chan, padded, 8 * width), BF16),
            pltpu.VMEM((n_chan, padded, 8 * width), BF16),
            pltpu.VMEM((baselines, LANES), F32),
            pltpu.VMEM((2 * baselines + 2 * rows, 8 * width), F32),
            pltpu.VMEM((baselines, 8 * width), BF16),
            pltpu.VMEM((n_tm, 8 * tile_rows, width), BF16),
            pltpu.VMEM((n_tm, 8 * tile_rows, width), BF16),
            dma((n_tm,)),
            dma((n_tm,)),
            dma((n_chan,)),
            dma((n_chan,)),
            dma((n_tm,)),
            dma((n_tm,)),
        ],
        compiler_params=pltpu.CompilerParams(
            collective_id=0, has_side_effects=True, vmem_limit_bytes=40 * 2**20
        ),
        cost_estimate=pl.CostEstimate(
            flops=2 * 10**8, bytes_accessed=2 * 10**6, transcendentals=0
        ),
    )(
        hbm(visibilities),
        hbm(station_gains),
        hbm(station_pairs.T),
        hbm(average_bands.T),
        hbm(tile_map.T),
        hbm(baseline_order.reshape(1, baselines)),
    )
    return pl.pallas_call(
        write_kernel,
        out_shape=(
            pltpu.HBM(averaged.shape, BF16),
            pltpu.HBM((tile_rows, 8, width), F32),
        ),
        in_specs=[vmem] * 2,
        out_specs=(pl.BlockSpec(memory_space=pltpu.HBM),) * 2,
        scratch_shapes=[pltpu.VMEM((tile_rows, 8, width), F32), dma((2,))],
        cost_estimate=pl.CostEstimate(flops=10**6, bytes_accessed=10**6, transcendentals=0),
    )(averaged, tiles)


def solution(mesh):
    n_tm, n_chan = mesh.shape["tm"], mesh.shape["chan"]
    tile_count = 8 * n_tm
    return jax.shard_map(
        functools.partial(shards, n_tm, n_chan, tile_count),
        mesh=mesh,
        in_specs=(P("tm", None, None, "chan"), P(None, "chan", None), P(), P(), P(), P()),
        out_specs=(P(None, None, "tm", "chan"), P("tm", None, "chan")),
        check_vma=False,
    )
```

```python
import functools

import jax
import jax.numpy as jnp
from jax import lax
from jax.experimental import pallas as pl
from jax.experimental.pallas import tpu as pltpu
from jax.sharding import PartitionSpec as P

TLOG = 3
CLOG = 2
LANES = 128
MESH = pl.DeviceIdType.MESH
F32 = jnp.float32
BF16 = jnp.bfloat16


def product(left, right):
    return (left[0] * right[0] - left[1] * right[1], left[0] * right[1] + left[1] * right[0])


def product_conj(left, right):
    return (left[0] * right[0] + left[1] * right[1], left[1] * right[0] - left[0] * right[1])


def add_pair(left, right):
    return (left[0] + right[0], left[1] + right[1])


def as_matrix(components):
    return [
        [(components[0], components[1]), (components[2], components[3])],
        [(components[4], components[5]), (components[6], components[7])],
    ]


def jones_apply(first, middle, second):
    left_gain = as_matrix(first)
    coherency = as_matrix(middle)
    right_gain = as_matrix(second)
    partial_rows = [
        [
            add_pair(
                product(left_gain[i][0], coherency[0][k]), product(left_gain[i][1], coherency[1][k])
            )
            for k in range(2)
        ]
        for i in range(2)
    ]
    result = []
    for i in range(2):
        for c in range(2):
            element = add_pair(
                product_conj(partial_rows[i][0], right_gain[c][0]),
                product_conj(partial_rows[i][1], right_gain[c][1]),
            )
            result.extend(element)
    return result


def split(values, width):
    return [values[:, i * width : (i + 1) * width] for i in range(8)]


def iota(shape, axis):
    return lax.broadcasted_iota(jnp.int32, shape, axis)


def dot(left, right):
    return jnp.dot(left, right, preferred_element_type=F32)


def one_hot(column, ids):
    return jnp.where(column == ids, 1.0, 0.0).astype(BF16)


def channel_means(width):
    row = iota((width, width), 0)
    column = iota((width, width), 1)
    means = []
    for level in range(1, CLOG + 1):
        same = (row >> level) == (column >> level)
        means.append(jnp.where(same, 2.0**-level, 0.0))
    return jnp.concatenate(means, axis=1).astype(BF16)


def channel_average(samples, means, level, width):
    averaged = dot(samples, means)
    result = samples.astype(F32)
    for k in range(1, CLOG + 1):
        result = jnp.where(level >= k, averaged[:, (k - 1) * width : k * width], result)
    return result


def kernel(
    n_tm, n_chan,
    vis_hbm, gain_hbm, pairs_hbm, bands_hbm, map_hbm, order_hbm, avg_ref, tiles_ref,
    vis_ref, gain_ref, pairs_ref, bands_ref, map_ref, order_ref, local, index,
    send, turned, gain_send, gains, table, chosen, calibrated, tiles_send, tiles,
    turn_out, turn_in, gain_out, gain_in, tile_out, tile_in,
):
    me = lax.axis_index("tm")
    mine = lax.axis_index("chan")
    baselines = vis_ref.shape[1]
    width = vis_ref.shape[2]
    rows = baselines // n_tm
    stations = gain_ref.shape[1]
    padded = gain_send.shape[1]
    tile_rows = tiles_ref.shape[1] // 8
    n_tiles = tile_rows * n_tm
    times = map_ref.shape[0]
    first_at, second_at, time_at, chan_at = range(times, times + 4)

    sources = (order_hbm, gain_hbm, vis_hbm.at[0], pairs_hbm, bands_hbm, map_hbm)
    targets = (order_ref, gain_ref, vis_ref, pairs_ref, bands_ref, map_ref)
    loads = [
        pltpu.make_async_copy(source, target, local.at[i])
        for i, (source, target) in enumerate(zip(sources, targets))
    ]
    for load in loads:
        load.start()

    barrier = pltpu.get_barrier_semaphore()
    for step in range(1, n_tm):
        pl.semaphore_signal(
            barrier, inc=1, device_id={"tm": lax.rem(me + step, n_tm)}, device_id_type=MESH
        )
    for step in range(1, n_chan):
        pl.semaphore_signal(
            barrier, inc=1, device_id={"chan": lax.rem(mine + step, n_chan)}, device_id_type=MESH
        )

    index[...] = jnp.zeros_like(index)
    loads[0].wait()
    place = jnp.where(order_ref[...] == iota((baselines, baselines), 0), 1.0, 0.0)
    loads[1].wait()
    for c in range(n_chan):
        block = jnp.concatenate(
            [gain_ref[i, :, c * width : (c + 1) * width] for i in range(8)], axis=1
        )
        if padded > stations:
            block = jnp.concatenate(
                [block, jnp.zeros((padded - stations, 8 * width), F32)], axis=0
            )
        gain_send[c] = block.astype(BF16)

    place = place.T.astype(BF16)
    loads[2].wait()
    raw = jnp.concatenate([vis_ref[i] for i in range(8)], axis=1)
    send[...] = dot(place, raw).astype(BF16).reshape(send.shape)

    pl.semaphore_wait(barrier, n_tm + n_chan - 2)

    copies = []
    gain_copies = []
    for step in range(1, n_chan):
        other = lax.rem(mine + step, n_chan)
        copy = pltpu.make_async_remote_copy(
            src_ref=gain_send.at[other],
            dst_ref=gains.at[mine],
            send_sem=gain_out.at[other],
            recv_sem=gain_in.at[mine],
            device_id={"chan": other},
            device_id_type=MESH,
        )
        copy.start()
        copies.append(copy)
    for step in range(1, n_tm):
        other = lax.rem(me + step, n_tm)
        copy = pltpu.make_async_remote_copy(
            src_ref=send.at[other],
            dst_ref=turned.at[me],
            send_sem=turn_out.at[other],
            recv_sem=turn_in.at[me],
            device_id={"tm": other},
            device_id_type=MESH,
        )
        copy.start()
        copies.append(copy)

    turned[me] = send[me]
    gains[mine] = gain_send[mine]
    means = channel_means(width)
    for load in loads[3:]:
        load.wait()
    index[:times] = map_ref[...].astype(F32)
    index[first_at : second_at + 1] = pairs_ref[...].astype(F32)
    index[time_at : chan_at + 1] = bands_ref[...].astype(F32)
    table[...] = lax.dot_general(
        place, index[...].astype(BF16), (((1,), (1,)), ((), ())), preferred_element_type=F32
    )

    ids = iota((1, n_chan * padded), 1)
    if padded > stations:
        lane = ids
        for c in range(n_chan):
            inside = (lane >= c * padded) & (lane < c * padded + stations)
            ids = jnp.where(inside, lane - c * (padded - stations), ids)
            ids = jnp.where((lane >= c * padded + stations) & (lane < (c + 1) * padded), -1, ids)
    here = pl.ds(pl.multiple_of(me * rows, rows), rows)
    at_all = table[...].astype(jnp.int32)
    at_here = table[here, :].astype(jnp.int32)
    pick = jnp.concatenate(
        [
            one_hot(at_all[:, first_at : first_at + 1], ids),
            one_hot(at_all[:, second_at : second_at + 1], ids),
            one_hot(at_here[:, first_at : first_at + 1], ids),
            one_hot(at_here[:, second_at : second_at + 1], ids),
        ],
        axis=0,
    )
    period = jnp.left_shift(jnp.ones((baselines, 1), jnp.int32), at_all[:, time_at : time_at + 1])
    start = me - (me & (period - 1))
    lane = iota((baselines, LANES), 1)
    tile = jnp.sum(
        jnp.where(lane == start, table[...], 0.0), axis=1, keepdims=True
    ).astype(jnp.int32)
    wide = max(n_tiles, LANES)
    share = jnp.where(
        tile == iota((baselines, wide), 1), 1.0 / period.astype(F32), 0.0
    )
    share = share.T[:n_tiles].astype(BF16)

    for step in range(1, n_chan):
        other = lax.rem(mine + step, n_chan)
        pltpu.make_async_remote_copy(
            src_ref=gain_send.at[other],
            dst_ref=gains.at[other],
            send_sem=gain_out.at[other],
            recv_sem=gain_in.at[other],
            device_id={"chan": other},
            device_id_type=MESH,
        ).wait_recv()
    chosen[...] = dot(pick, gains[...].reshape(n_chan * padded, 8 * width))

    def calibrate_block(k, carry):
        at = pl.ds(pl.multiple_of(k * rows, rows), rows)
        at_second = pl.ds(pl.multiple_of(baselines + k * rows, rows), rows)
        result = jones_apply(
            split(chosen[at, :], width),
            split(send[k].astype(F32), width),
            split(chosen[at_second, :], width),
        )
        calibrated[at, :] = jnp.concatenate(result, axis=1).astype(BF16)
        return carry

    lax.fori_loop(0, n_tm, calibrate_block, 0, unroll=2)
    level = at_all[:, chan_at : chan_at + 1]
    sums = []
    for i in range(8):
        part = channel_average(calibrated[:, i * width : (i + 1) * width], means, level, width)
        sums.append(dot(share, part.astype(BF16)).reshape(n_tm, tile_rows, width))
    tiles_send[...] = jnp.concatenate(sums, axis=1).astype(BF16)
    for step in range(1, n_tm):
        other = lax.rem(me + step, n_tm)
        copy = pltpu.make_async_remote_copy(
            src_ref=tiles_send.at[other],
            dst_ref=tiles.at[me],
            send_sem=tile_out.at[other],
            recv_sem=tile_in.at[me],
            device_id={"tm": other},
            device_id_type=MESH,
        )
        copy.start()
        copies.append(copy)
    tiles[me] = tiles_send[me]

    for step in range(1, n_tm):
        other = lax.rem(me + step, n_tm)
        pltpu.make_async_remote_copy(
            src_ref=send.at[other],
            dst_ref=turned.at[other],
            send_sem=turn_out.at[other],
            recv_sem=turn_in.at[other],
            device_id={"tm": other},
            device_id_type=MESH,
        ).wait_recv()
    left = split(chosen[2 * baselines : 2 * baselines + rows, :], width)
    right = split(chosen[2 * baselines + rows : 2 * baselines + 2 * rows, :], width)

    def calibrate_time(t, carry):
        result = jones_apply(left, split(turned[t].astype(F32), width), right)
        at = pl.ds(pl.multiple_of(t * rows, rows), rows)
        calibrated[at, :] = jnp.concatenate(result, axis=1).astype(BF16)
        return carry

    lax.fori_loop(0, n_tm, calibrate_time, 0, unroll=2)
    group = 2**TLOG
    time_level = jnp.broadcast_to(at_here[:, time_at : time_at + 1], (rows, width))
    chan_level = jnp.broadcast_to(at_here[:, chan_at : chan_at + 1], (rows, width))
    chan_level = jnp.concatenate([chan_level] * group, axis=0)
    for first in range(0, n_tm, group):
        at = slice(first * rows, (first + group) * rows)
        for i in range(8):
            part = channel_average(
                calibrated[at, i * width : (i + 1) * width], means, chan_level, width
            )
            current = [part[t * rows : (t + 1) * rows] for t in range(group)]
            result = list(current)
            for k in range(1, TLOG + 1):
                current = [
                    0.5 * (current[2 * j] + current[2 * j + 1]) for j in range(len(current) // 2)
                ]
                result = [
                    jnp.where(time_level >= k, current[t >> k], result[t]) for t in range(group)
                ]
            for t in range(group):
                avg_ref[first + t, i] = result[t].astype(BF16)

    for step in range(1, n_tm):
        other = lax.rem(me + step, n_tm)
        pltpu.make_async_remote_copy(
            src_ref=tiles_send.at[other],
            dst_ref=tiles.at[other],
            send_sem=tile_out.at[other],
            recv_sem=tile_in.at[other],
            device_id={"tm": other},
            device_id_type=MESH,
        ).wait_recv()
    tiles_ref[...] = tiles[...]
    for copy in copies:
        copy.wait_send()


def write_kernel(avg_ref, tiles_ref, avg_hbm, grid_hbm, grid, done):
    averaged = pltpu.make_async_copy(avg_ref, avg_hbm, done.at[0])
    averaged.start()
    tile_rows = grid.shape[0]
    total = tiles_ref[0].astype(F32)
    for m in range(1, tiles_ref.shape[0]):
        total = total + tiles_ref[m].astype(F32)
    for i in range(8):
        grid[:, i, :] = total[i * tile_rows : (i + 1) * tile_rows]
    gridded = pltpu.make_async_copy(grid, grid_hbm, done.at[1])
    gridded.start()
    averaged.wait()
    gridded.wait()


def shards(n_tm, n_chan, tile_count, visibilities, station_gains, station_pairs, average_bands, tile_map, baseline_order):
    baselines, width = visibilities.shape[2:]
    rows = baselines // n_tm
    stations = station_gains.shape[1]
    padded = -(-stations // 16) * 16
    tile_rows = tile_count // n_tm
    vmem = pl.BlockSpec(memory_space=pltpu.VMEM)
    dma = pltpu.SemaphoreType.DMA
    hbm = functools.partial(pltpu.with_memory_space_constraint, memory_space=pltpu.HBM)
    near = functools.partial(pltpu.with_memory_space_constraint, memory_space=pltpu.VMEM)
    averaged, tiles = pl.pallas_call(
        functools.partial(kernel, n_tm, n_chan),
        out_shape=(
            pltpu.VMEM((n_tm, 8, rows, width), BF16),
            pltpu.VMEM((n_tm, 8 * tile_rows, width), BF16),
        ),
        in_specs=[pl.BlockSpec(memory_space=pl.ANY)] * 6,
        out_specs=(vmem, vmem),
        scratch_shapes=[
            pltpu.VMEM((8, baselines, width), BF16),
            pltpu.VMEM(station_gains.shape, F32),
            pltpu.VMEM((2, baselines), jnp.int32),
            pltpu.VMEM((2, baselines), jnp.int32),
            pltpu.VMEM((n_tm, baselines), jnp.int32),
            pltpu.VMEM((1, baselines), jnp.int32),
            dma((6,)),
            pltpu.VMEM((LANES, baselines), F32),
            pltpu.VMEM((n_tm, rows, 8 * width), BF16),
            pltpu.VMEM((n_tm, rows, 8 * width), BF16),
            pltpu.VMEM((n_chan, padded, 8 * width), BF16),
            pltpu.VMEM((n_chan, padded, 8 * width), BF16),
            pltpu.VMEM((baselines, LANES), F32),
            pltpu.VMEM((2 * baselines + 2 * rows, 8 * width), F32),
            pltpu.VMEM((baselines, 8 * width), BF16),
            pltpu.VMEM((n_tm, 8 * tile_rows, width), BF16),
            pltpu.VMEM((n_tm, 8 * tile_rows, width), BF16),
            dma((n_tm,)),
            dma((n_tm,)),
            dma((n_chan,)),
            dma((n_chan,)),
            dma((n_tm,)),
            dma((n_tm,)),
        ],
        compiler_params=pltpu.CompilerParams(
            collective_id=0, has_side_effects=True, vmem_limit_bytes=40 * 2**20
        ),
        cost_estimate=pl.CostEstimate(
            flops=2 * 10**8, bytes_accessed=2 * 10**6, transcendentals=0
        ),
    )(
        hbm(visibilities),
        hbm(station_gains),
        hbm(station_pairs.T),
        hbm(average_bands.T),
        hbm(tile_map.T),
        hbm(baseline_order.reshape(1, baselines)),
    )
    return pl.pallas_call(
        write_kernel,
        out_shape=(
            pltpu.HBM(averaged.shape, BF16),
            pltpu.HBM((tile_rows, 8, width), F32),
        ),
        in_specs=[vmem] * 2,
        out_specs=(pl.BlockSpec(memory_space=pltpu.HBM),) * 2,
        scratch_shapes=[pltpu.VMEM((tile_rows, 8, width), F32), dma((2,))],
        compiler_params=pltpu.CompilerParams(vmem_limit_bytes=8 * 2**20),
        cost_estimate=pl.CostEstimate(flops=10**6, bytes_accessed=10**6, transcendentals=0),
    )(near(averaged), near(tiles))


def solution(mesh):
    n_tm, n_chan = mesh.shape["tm"], mesh.shape["chan"]
    tile_count = 8 * n_tm
    return jax.shard_map(
        functools.partial(shards, n_tm, n_chan, tile_count),
        mesh=mesh,
        in_specs=(P("tm", None, None, "chan"), P(None, "chan", None), P(), P(), P(), P()),
        out_specs=(P(None, None, "tm", "chan"), P("tm", None, "chan")),
        check_vma=False,
    )
```

```python
import functools

import jax
import jax.numpy as jnp
from jax import lax
from jax.experimental import pallas as pl
from jax.experimental.pallas import tpu as pltpu
from jax.sharding import PartitionSpec as P

TLOG = 3
CLOG = 2
LANES = 128
MESH = pl.DeviceIdType.MESH
F32 = jnp.float32
BF16 = jnp.bfloat16


def product(left, right):
    return (left[0] * right[0] - left[1] * right[1], left[0] * right[1] + left[1] * right[0])


def product_conj(left, right):
    return (left[0] * right[0] + left[1] * right[1], left[1] * right[0] - left[0] * right[1])


def add_pair(left, right):
    return (left[0] + right[0], left[1] + right[1])


def as_matrix(components):
    return [
        [(components[0], components[1]), (components[2], components[3])],
        [(components[4], components[5]), (components[6], components[7])],
    ]


def jones_apply(first, middle, second):
    left_gain = as_matrix(first)
    coherency = as_matrix(middle)
    right_gain = as_matrix(second)
    partial_rows = [
        [
            add_pair(
                product(left_gain[i][0], coherency[0][k]), product(left_gain[i][1], coherency[1][k])
            )
            for k in range(2)
        ]
        for i in range(2)
    ]
    result = []
    for i in range(2):
        for c in range(2):
            element = add_pair(
                product_conj(partial_rows[i][0], right_gain[c][0]),
                product_conj(partial_rows[i][1], right_gain[c][1]),
            )
            result.extend(element)
    return result


def split(values, width):
    return [values[:, i * width : (i + 1) * width] for i in range(values.shape[1] // width)]


def iota(shape, axis):
    return lax.broadcasted_iota(jnp.int32, shape, axis)


def dot(left, right):
    return jnp.dot(left, right, preferred_element_type=F32)


def one_hot(column, ids):
    return jnp.where(column == ids, 1.0, 0.0).astype(BF16)


def channel_means(width):
    row = iota((width, width), 0)
    column = iota((width, width), 1)
    means = []
    for level in range(1, CLOG + 1):
        same = (row >> level) == (column >> level)
        means.append(jnp.where(same, 2.0**-level, 0.0))
    return jnp.concatenate(means, axis=1).astype(BF16)


def row_times(row, middle):
    return [
        add_pair(product(row[0], middle[0][b]), product(row[1], middle[1][b])) for b in range(2)
    ]


def times_row_conj(partial, row):
    return add_pair(product_conj(partial[0], row[0]), product_conj(partial[1], row[1]))


def as_row(components):
    return [(components[0], components[1]), (components[2], components[3])]


def flat(pairs):
    return jnp.concatenate([part for pair in pairs for part in pair], axis=1)


def tile_sums(share, samples, means, blocks, width):
    count = samples.shape[1] // width
    summed = dot(share, samples)
    n_tiles = share.shape[0] // (CLOG + 1)
    levels = []
    for i in range(count):
        part = summed[:, i * width : (i + 1) * width]
        levels.append(
            jnp.concatenate(
                [part[k * n_tiles : (k + 1) * n_tiles] for k in range(1, CLOG + 1)], axis=1
            )
        )
    spread = dot(jnp.concatenate(levels, axis=0).astype(BF16), means)
    result = []
    for i in range(count):
        part = summed[:n_tiles, i * width : (i + 1) * width]
        part = part + spread[i * n_tiles : (i + 1) * n_tiles]
        result.append(part.reshape(blocks, n_tiles // blocks, width))
    return jnp.concatenate(result, axis=1).astype(BF16)


def channel_average(samples, means, level, width):
    averaged = dot(samples, means)
    result = samples.astype(F32)
    for k in range(1, CLOG + 1):
        result = jnp.where(level >= k, averaged[:, (k - 1) * width : k * width], result)
    return result


def peers(mine, count):
    chips = count // 2
    chip = mine // 2
    core = lax.rem(mine, 2)
    others = []
    for step in range(1, chips):
        for flip in range(2):
            others.append(lax.rem(chip + step, chips) * 2 + lax.rem(core + flip, 2))
    return others + [chip * 2 + 1 - core]


def kernel(
    n_tm, n_chan,
    vis_hbm, gain_hbm, pairs_hbm, bands_hbm, map_hbm, order_hbm, avg_ref, early_tiles, late_tiles,
    vis_ref, gain_ref, pairs_ref, bands_ref, map_ref, order_ref, local, index,
    send, turned, gain_send, gains, table, chosen, partials, calibrated, early_send, late_send,
    turn_out, turn_in, gain_out, gain_in, tile_out, tile_in,
):
    me = lax.axis_index("tm")
    mine = lax.axis_index("chan")
    baselines = vis_ref.shape[1]
    width = vis_ref.shape[2]
    rows = baselines // n_tm
    stations = gain_ref.shape[1]
    padded = gain_send.shape[2]
    tile_rows = early_tiles.shape[1] // 2
    n_tiles = tile_rows * n_tm
    times = map_ref.shape[0]
    first_at, second_at, time_at, chan_at = range(times, times + 4)
    around = [lax.rem(me + step, n_tm) for step in range(1, n_tm)]
    across = peers(mine, n_chan)

    sources = (
        gain_hbm.at[0:4], order_hbm, gain_hbm.at[4:8], vis_hbm.at[0], pairs_hbm, bands_hbm, map_hbm
    )
    targets = (
        gain_ref.at[0:4], order_ref, gain_ref.at[4:8], vis_ref, pairs_ref, bands_ref, map_ref
    )
    loads = [
        pltpu.make_async_copy(source, target, local.at[i])
        for i, (source, target) in enumerate(zip(sources, targets))
    ]
    for load in loads:
        load.start()

    barrier = pltpu.get_barrier_semaphore()
    for other in around:
        pl.semaphore_signal(barrier, inc=1, device_id={"tm": other}, device_id_type=MESH)
    for other in across:
        pl.semaphore_signal(barrier, inc=1, device_id={"chan": other}, device_id_type=MESH)

    def pack_gains(half):
        for c in range(n_chan):
            block = jnp.concatenate(
                [
                    gain_ref[4 * half + i, :, c * width : (c + 1) * width] for i in range(4)
                ],
                axis=1,
            )
            if padded > stations:
                block = jnp.concatenate(
                    [block, jnp.zeros((padded - stations, 4 * width), F32)], axis=0
                )
            gain_send[half, c] = block.astype(BF16)

    def gain_copy(half, other, slot):
        return pltpu.make_async_remote_copy(
            src_ref=gain_send.at[half, other],
            dst_ref=gains.at[half, slot],
            send_sem=gain_out.at[half, other],
            recv_sem=gain_in.at[half, slot],
            device_id={"chan": other},
            device_id_type=MESH,
        )

    def turn_copy(other, slot):
        return pltpu.make_async_remote_copy(
            src_ref=send.at[other],
            dst_ref=turned.at[slot],
            send_sem=turn_out.at[other],
            recv_sem=turn_in.at[slot],
            device_id={"tm": other},
            device_id_type=MESH,
        )

    def tile_copy(chunk, other, slot):
        source, target = ((early_send, early_tiles), (late_send, late_tiles))[chunk]
        return pltpu.make_async_remote_copy(
            src_ref=source.at[other],
            dst_ref=target.at[slot],
            send_sem=tile_out.at[chunk, other],
            recv_sem=tile_in.at[chunk, slot],
            device_id={"tm": other},
            device_id_type=MESH,
        )

    copies = []

    def start(copy):
        copy.start()
        copies.append(copy)

    loads[0].wait()
    pack_gains(0)
    loads[1].wait()
    place = jnp.where(order_ref[...] == iota((baselines, baselines), 0), 1.0, 0.0)
    place = place.T.astype(BF16)

    pl.semaphore_wait(barrier, n_tm + n_chan - 2)

    for other in across:
        start(gain_copy(0, other, mine))
    loads[2].wait()
    pack_gains(1)
    for other in across:
        start(gain_copy(1, other, mine))

    loads[3].wait()
    raw = jnp.concatenate([vis_ref[i] for i in range(8)], axis=1)
    send[...] = dot(place, raw).astype(BF16).reshape(send.shape)
    for other in around:
        start(turn_copy(other, me))

    turned[me] = send[me]
    gains[0, mine] = gain_send[0, mine]
    gains[1, mine] = gain_send[1, mine]
    means = channel_means(width)
    stacked = jnp.concatenate(
        [means[:, k * width : (k + 1) * width] for k in range(CLOG)], axis=0
    )
    for load in loads[4:]:
        load.wait()
    index[...] = jnp.zeros_like(index)
    index[:times] = map_ref[...].astype(F32)
    index[first_at : second_at + 1] = pairs_ref[...].astype(F32)
    index[time_at : chan_at + 1] = bands_ref[...].astype(F32)
    table[...] = lax.dot_general(
        place, index[...].astype(BF16), (((1,), (1,)), ((), ())), preferred_element_type=F32
    )

    ids = iota((1, n_chan * padded), 1)
    if padded > stations:
        lane = ids
        for c in range(n_chan):
            inside = (lane >= c * padded) & (lane < c * padded + stations)
            ids = jnp.where(inside, lane - c * (padded - stations), ids)
            ids = jnp.where((lane >= c * padded + stations) & (lane < (c + 1) * padded), -1, ids)
    here = pl.ds(pl.multiple_of(me * rows, rows), rows)
    at_all = table[...].astype(jnp.int32)
    at_here = table[here, :].astype(jnp.int32)
    pick = jnp.concatenate(
        [
            one_hot(at_all[:, first_at : first_at + 1], ids),
            one_hot(at_all[:, second_at : second_at + 1], ids),
            one_hot(at_here[:, first_at : first_at + 1], ids),
            one_hot(at_here[:, second_at : second_at + 1], ids),
        ],
        axis=0,
    )
    period = jnp.left_shift(jnp.ones((baselines, 1), jnp.int32), at_all[:, time_at : time_at + 1])
    begin = me - (me & (period - 1))
    lane = iota((baselines, LANES), 1)
    tile = jnp.sum(
        jnp.where(lane == begin, table[...], 0.0), axis=1, keepdims=True
    ).astype(jnp.int32)
    tile = tile + n_tiles * at_all[:, chan_at : chan_at + 1]
    n_share = (CLOG + 1) * n_tiles
    wide = -(-n_share // LANES) * LANES
    share = jnp.where(tile == iota((baselines, wide), 1), 1.0 / period.astype(F32), 0.0)
    share = share.T[:n_share].astype(BF16)

    def block_rows(k):
        at = pl.ds(pl.multiple_of(k * rows, rows), rows)
        return at, pl.ds(pl.multiple_of(baselines + k * rows, rows), rows)

    for other in across:
        gain_copy(0, other, other).wait_recv()
    chosen[0] = dot(pick, gains[0].reshape(n_chan * padded, 4 * width))

    def calibrate_early(k, carry):
        at, at_second = block_rows(k)
        coherency = as_matrix(split(send[k].astype(F32), width))
        partial = row_times(as_row(split(chosen[0, at, :], width)), coherency)
        partials[at, :] = flat(partial)
        entry = times_row_conj(partial, as_row(split(chosen[0, at_second, :], width)))
        calibrated[at, : 2 * width] = flat([entry]).astype(BF16)
        return carry

    lax.fori_loop(0, n_tm, calibrate_early, 0, unroll=2)
    early_send[...] = tile_sums(share, calibrated[:, : 2 * width], stacked, n_tm, width)
    for other in around:
        start(tile_copy(0, other, me))
    early_tiles[me] = early_send[me]

    for other in across:
        gain_copy(1, other, other).wait_recv()
    chosen[1] = dot(pick, gains[1].reshape(n_chan * padded, 4 * width))

    def calibrate_late(k, carry):
        at, at_second = block_rows(k)
        coherency = as_matrix(split(send[k].astype(F32), width))
        upper = as_row(split(partials[at, :], width))
        lower = row_times(as_row(split(chosen[1, at, :], width)), coherency)
        right_upper = as_row(split(chosen[0, at_second, :], width))
        right_lower = as_row(split(chosen[1, at_second, :], width))
        entries = [
            times_row_conj(upper, right_lower),
            times_row_conj(lower, right_upper),
            times_row_conj(lower, right_lower),
        ]
        calibrated[at, 2 * width :] = flat(entries).astype(BF16)
        return carry

    lax.fori_loop(0, n_tm, calibrate_late, 0, unroll=2)
    late_send[...] = tile_sums(share, calibrated[:, 2 * width :], stacked, n_tm, width)
    for other in around:
        start(tile_copy(1, other, me))
    late_tiles[me] = late_send[me]

    for other in around:
        turn_copy(other, other).wait_recv()
    ends = (2 * baselines, 2 * baselines + rows, 2 * baselines + 2 * rows)
    left, right = [
        split(chosen[0, ends[j] : ends[j + 1], :], width)
        + split(chosen[1, ends[j] : ends[j + 1], :], width)
        for j in range(2)
    ]

    def calibrate_time(t, carry):
        result = jones_apply(left, split(turned[t].astype(F32), width), right)
        at = pl.ds(pl.multiple_of(t * rows, rows), rows)
        calibrated[at, :] = jnp.concatenate(result, axis=1).astype(BF16)
        return carry

    lax.fori_loop(0, n_tm, calibrate_time, 0, unroll=2)
    group = 2**TLOG
    time_level = jnp.broadcast_to(at_here[:, time_at : time_at + 1], (rows, width))
    chan_level = jnp.broadcast_to(at_here[:, chan_at : chan_at + 1], (rows, width))
    chan_level = jnp.concatenate([chan_level] * group, axis=0)
    for first in range(0, n_tm, group):
        at = slice(first * rows, (first + group) * rows)
        for i in range(8):
            part = channel_average(
                calibrated[at, i * width : (i + 1) * width], means, chan_level, width
            )
            current = [part[t * rows : (t + 1) * rows] for t in range(group)]
            result = list(current)
            for k in range(1, TLOG + 1):
                current = [
                    0.5 * (current[2 * j] + current[2 * j + 1]) for j in range(len(current) // 2)
                ]
                result = [
                    jnp.where(time_level >= k, current[t >> k], result[t]) for t in range(group)
                ]
            for t in range(group):
                avg_ref[first + t, i] = result[t].astype(BF16)

    for chunk in range(2):
        for other in around:
            tile_copy(chunk, other, other).wait_recv()
    for copy in copies:
        copy.wait_send()


def write_kernel(avg_ref, early_ref, late_ref, avg_hbm, grid_hbm, grid, done):
    averaged = pltpu.make_async_copy(avg_ref, avg_hbm, done.at[0])
    averaged.start()
    tile_rows = grid.shape[0]
    first = 0
    for ref in (early_ref, late_ref):
        total = ref[0].astype(F32)
        for m in range(1, ref.shape[0]):
            total = total + ref[m].astype(F32)
        count = ref.shape[1] // tile_rows
        for i in range(count):
            grid[:, first + i, :] = total[i * tile_rows : (i + 1) * tile_rows]
        first += count
    gridded = pltpu.make_async_copy(grid, grid_hbm, done.at[1])
    gridded.start()
    averaged.wait()
    gridded.wait()


def shards(n_tm, n_chan, tile_count, visibilities, station_gains, station_pairs, average_bands, tile_map, baseline_order):
    baselines, width = visibilities.shape[2:]
    rows = baselines // n_tm
    stations = station_gains.shape[1]
    padded = -(-stations // 16) * 16
    tile_rows = tile_count // n_tm
    vmem = pl.BlockSpec(memory_space=pltpu.VMEM)
    dma = pltpu.SemaphoreType.DMA
    hbm = functools.partial(pltpu.with_memory_space_constraint, memory_space=pltpu.HBM)
    near = functools.partial(pltpu.with_memory_space_constraint, memory_space=pltpu.VMEM)
    averaged, early, late = pl.pallas_call(
        functools.partial(kernel, n_tm, n_chan),
        out_shape=(
            pltpu.VMEM((n_tm, 8, rows, width), BF16),
            pltpu.VMEM((n_tm, 2 * tile_rows, width), BF16),
            pltpu.VMEM((n_tm, 6 * tile_rows, width), BF16),
        ),
        in_specs=[pl.BlockSpec(memory_space=pl.ANY)] * 6,
        out_specs=(vmem,) * 3,
        scratch_shapes=[
            pltpu.VMEM((8, baselines, width), BF16),
            pltpu.VMEM(station_gains.shape, F32),
            pltpu.VMEM((2, baselines), jnp.int32),
            pltpu.VMEM((2, baselines), jnp.int32),
            pltpu.VMEM((n_tm, baselines), jnp.int32),
            pltpu.VMEM((1, baselines), jnp.int32),
            dma((7,)),
            pltpu.VMEM((LANES, baselines), F32),
            pltpu.VMEM((n_tm, rows, 8 * width), BF16),
            pltpu.VMEM((n_tm, rows, 8 * width), BF16),
            pltpu.VMEM((2, n_chan, padded, 4 * width), BF16),
            pltpu.VMEM((2, n_chan, padded, 4 * width), BF16),
            pltpu.VMEM((baselines, LANES), F32),
            pltpu.VMEM((2, 2 * baselines + 2 * rows, 4 * width), F32),
            pltpu.VMEM((baselines, 4 * width), F32),
            pltpu.VMEM((baselines, 8 * width), BF16),
            pltpu.VMEM((n_tm, 2 * tile_rows, width), BF16),
            pltpu.VMEM((n_tm, 6 * tile_rows, width), BF16),
            dma((n_tm,)),
            dma((n_tm,)),
            dma((2, n_chan)),
            dma((2, n_chan)),
            dma((2, n_tm)),
            dma((2, n_tm)),
        ],
        compiler_params=pltpu.CompilerParams(
            collective_id=0, has_side_effects=True, vmem_limit_bytes=40 * 2**20
        ),
        cost_estimate=pl.CostEstimate(
            flops=2 * 10**8, bytes_accessed=2 * 10**6, transcendentals=0
        ),
    )(
        hbm(visibilities),
        hbm(station_gains),
        hbm(station_pairs.T),
        hbm(average_bands.T),
        hbm(tile_map.T),
        hbm(baseline_order.reshape(1, baselines)),
    )
    return pl.pallas_call(
        write_kernel,
        out_shape=(
            pltpu.HBM(averaged.shape, BF16),
            pltpu.HBM((tile_rows, 8, width), F32),
        ),
        in_specs=[vmem] * 3,
        out_specs=(pl.BlockSpec(memory_space=pltpu.HBM),) * 2,
        scratch_shapes=[pltpu.VMEM((tile_rows, 8, width), F32), dma((2,))],
        compiler_params=pltpu.CompilerParams(vmem_limit_bytes=8 * 2**20),
        cost_estimate=pl.CostEstimate(flops=10**6, bytes_accessed=10**6, transcendentals=0),
    )(near(averaged), near(early), near(late))


def solution(mesh):
    n_tm, n_chan = mesh.shape["tm"], mesh.shape["chan"]
    tile_count = 8 * n_tm
    return jax.shard_map(
        functools.partial(shards, n_tm, n_chan, tile_count),
        mesh=mesh,
        in_specs=(P("tm", None, None, "chan"), P(None, "chan", None), P(), P(), P(), P()),
        out_specs=(P(None, None, "tm", "chan"), P("tm", None, "chan")),
        check_vma=False,
    )
```

```python
import functools

import jax
import jax.numpy as jnp
from jax import lax
from jax.experimental import pallas as pl
from jax.experimental.pallas import tpu as pltpu
from jax.sharding import PartitionSpec as P

TLOG = 3
CLOG = 2
LANES = 128
MESH = pl.DeviceIdType.MESH
F32 = jnp.float32
BF16 = jnp.bfloat16


def product(left, right):
    return (left[0] * right[0] - left[1] * right[1], left[0] * right[1] + left[1] * right[0])


def product_conj(left, right):
    return (left[0] * right[0] + left[1] * right[1], left[1] * right[0] - left[0] * right[1])


def add_pair(left, right):
    return (left[0] + right[0], left[1] + right[1])


def as_matrix(components):
    return [
        [(components[0], components[1]), (components[2], components[3])],
        [(components[4], components[5]), (components[6], components[7])],
    ]


def jones_apply(first, middle, second):
    left_gain = as_matrix(first)
    coherency = as_matrix(middle)
    right_gain = as_matrix(second)
    partial_rows = [
        [
            add_pair(
                product(left_gain[i][0], coherency[0][k]), product(left_gain[i][1], coherency[1][k])
            )
            for k in range(2)
        ]
        for i in range(2)
    ]
    result = []
    for i in range(2):
        for c in range(2):
            element = add_pair(
                product_conj(partial_rows[i][0], right_gain[c][0]),
                product_conj(partial_rows[i][1], right_gain[c][1]),
            )
            result.extend(element)
    return result


def split(values, width):
    return [values[:, i * width : (i + 1) * width] for i in range(values.shape[1] // width)]


def iota(shape, axis):
    return lax.broadcasted_iota(jnp.int32, shape, axis)


def dot(left, right):
    return jnp.dot(left, right, preferred_element_type=F32)


def one_hot(column, ids):
    return jnp.where(column == ids, 1.0, 0.0).astype(BF16)


def channel_means(width):
    row = iota((width, width), 0)
    column = iota((width, width), 1)
    means = []
    for level in range(1, CLOG + 1):
        same = (row >> level) == (column >> level)
        means.append(jnp.where(same, 2.0**-level, 0.0))
    return jnp.concatenate(means, axis=1).astype(BF16)


def row_times(row, middle):
    return [
        add_pair(product(row[0], middle[0][b]), product(row[1], middle[1][b])) for b in range(2)
    ]


def times_row_conj(partial, row):
    return add_pair(product_conj(partial[0], row[0]), product_conj(partial[1], row[1]))


def as_row(components):
    return [(components[0], components[1]), (components[2], components[3])]


def flat(pairs):
    return jnp.concatenate([part for pair in pairs for part in pair], axis=1)


def tile_sums(share, samples, means, blocks, width):
    count = samples.shape[1] // width
    summed = dot(share, samples)
    n_tiles = share.shape[0] // (CLOG + 1)
    levels = []
    for i in range(count):
        part = summed[:, i * width : (i + 1) * width]
        levels.append(
            jnp.concatenate(
                [part[k * n_tiles : (k + 1) * n_tiles] for k in range(1, CLOG + 1)], axis=1
            )
        )
    spread = dot(jnp.concatenate(levels, axis=0).astype(BF16), means)
    result = []
    for i in range(count):
        part = summed[:n_tiles, i * width : (i + 1) * width]
        part = part + spread[i * n_tiles : (i + 1) * n_tiles]
        result.append(part.reshape(blocks, n_tiles // blocks, width))
    return jnp.concatenate(result, axis=1).astype(BF16)


def channel_average(samples, means, level, width):
    averaged = dot(samples, means)
    result = samples.astype(F32)
    for k in range(1, CLOG + 1):
        result = jnp.where(level >= k, averaged[:, (k - 1) * width : k * width], result)
    return result


def peers(mine, count):
    chips = count // 2
    chip = mine // 2
    core = lax.rem(mine, 2)
    others = []
    for step in range(1, chips):
        for flip in range(2):
            others.append(lax.rem(chip + step, chips) * 2 + lax.rem(core + flip, 2))
    return others + [chip * 2 + 1 - core]


def kernel(
    n_tm, n_chan,
    vis_hbm, gain_hbm, pairs_hbm, bands_hbm, map_hbm, order_hbm, avg_ref, early_tiles, late_tiles,
    vis_ref, gain_ref, pairs_ref, bands_ref, map_ref, order_ref, local, index,
    send, turned, gain_send, gains, table, chosen, partials, calibrated, early_send, late_send,
    turn_out, turn_in, gain_out, gain_in, tile_out, tile_in,
):
    me = lax.axis_index("tm")
    mine = lax.axis_index("chan")
    baselines = vis_ref.shape[1]
    width = vis_ref.shape[2]
    rows = baselines // n_tm
    stations = gain_ref.shape[1]
    padded = gain_send.shape[2]
    tile_rows = early_tiles.shape[1] // 2
    n_tiles = tile_rows * n_tm
    times = map_ref.shape[0]
    first_at, second_at, time_at, chan_at = range(times, times + 4)
    around = [step + lax.div(step - me + n_tm, n_tm) for step in range(n_tm - 1)]
    across = peers(mine, n_chan)

    sources = (
        gain_hbm.at[0:4], order_hbm, gain_hbm.at[4:8], vis_hbm.at[0], pairs_hbm, bands_hbm, map_hbm
    )
    targets = (
        gain_ref.at[0:4], order_ref, gain_ref.at[4:8], vis_ref, pairs_ref, bands_ref, map_ref
    )
    loads = [
        pltpu.make_async_copy(source, target, local.at[i])
        for i, (source, target) in enumerate(zip(sources, targets))
    ]
    for load in loads:
        load.start()

    barrier = pltpu.get_barrier_semaphore()
    for other in around:
        pl.semaphore_signal(barrier, inc=1, device_id={"tm": other}, device_id_type=MESH)
    for other in across:
        pl.semaphore_signal(barrier, inc=1, device_id={"chan": other}, device_id_type=MESH)

    def pack_gains(half):
        for c in range(n_chan):
            block = jnp.concatenate(
                [
                    gain_ref[4 * half + i, :, c * width : (c + 1) * width] for i in range(4)
                ],
                axis=1,
            )
            if padded > stations:
                block = jnp.concatenate(
                    [block, jnp.zeros((padded - stations, 4 * width), F32)], axis=0
                )
            gain_send[half, c] = block.astype(BF16)

    def gain_copy(half, other, slot):
        return pltpu.make_async_remote_copy(
            src_ref=gain_send.at[half, other],
            dst_ref=gains.at[half, slot],
            send_sem=gain_out.at[half, other],
            recv_sem=gain_in.at[half, slot],
            device_id={"chan": other},
            device_id_type=MESH,
        )

    def turn_copy(other, slot):
        return pltpu.make_async_remote_copy(
            src_ref=send.at[other],
            dst_ref=turned.at[slot],
            send_sem=turn_out.at[other],
            recv_sem=turn_in.at[slot],
            device_id={"tm": other},
            device_id_type=MESH,
        )

    def tile_copy(chunk, other, slot):
        source, target = ((early_send, early_tiles), (late_send, late_tiles))[chunk]
        return pltpu.make_async_remote_copy(
            src_ref=source.at[other],
            dst_ref=target.at[slot],
            send_sem=tile_out.at[chunk, other],
            recv_sem=tile_in.at[chunk, slot],
            device_id={"tm": other},
            device_id_type=MESH,
        )

    copies = []

    def start(copy):
        copy.start()
        copies.append(copy)

    loads[0].wait()
    pack_gains(0)
    loads[1].wait()
    place = jnp.where(order_ref[...] == iota((baselines, baselines), 0), 1.0, 0.0)
    place = place.T.astype(BF16)

    pl.semaphore_wait(barrier, n_tm + n_chan - 2)

    for other in across:
        start(gain_copy(0, other, mine))
    loads[2].wait()
    pack_gains(1)
    for other in across:
        start(gain_copy(1, other, mine))

    loads[3].wait()
    raw = jnp.concatenate([vis_ref[i] for i in range(8)], axis=1)
    send[...] = dot(place, raw).astype(BF16).reshape(send.shape)
    for other in around:
        start(turn_copy(other, me))

    turned[me] = send[me]
    gains[0, mine] = gain_send[0, mine]
    gains[1, mine] = gain_send[1, mine]
    means = channel_means(width)
    stacked = jnp.concatenate(
        [means[:, k * width : (k + 1) * width] for k in range(CLOG)], axis=0
    )
    for load in loads[4:]:
        load.wait()
    index[...] = jnp.zeros_like(index)
    index[:times] = map_ref[...].astype(F32)
    index[first_at : second_at + 1] = pairs_ref[...].astype(F32)
    index[time_at : chan_at + 1] = bands_ref[...].astype(F32)
    table[...] = lax.dot_general(
        place, index[...].astype(BF16), (((1,), (1,)), ((), ())), preferred_element_type=F32
    )

    ids = iota((1, n_chan * padded), 1)
    if padded > stations:
        lane = ids
        for c in range(n_chan):
            inside = (lane >= c * padded) & (lane < c * padded + stations)
            ids = jnp.where(inside, lane - c * (padded - stations), ids)
            ids = jnp.where((lane >= c * padded + stations) & (lane < (c + 1) * padded), -1, ids)
    here = pl.ds(pl.multiple_of(me * rows, rows), rows)
    at_all = table[...].astype(jnp.int32)
    at_here = table[here, :].astype(jnp.int32)
    pick = jnp.concatenate(
        [
            one_hot(at_all[:, first_at : first_at + 1], ids),
            one_hot(at_all[:, second_at : second_at + 1], ids),
            one_hot(at_here[:, first_at : first_at + 1], ids),
            one_hot(at_here[:, second_at : second_at + 1], ids),
        ],
        axis=0,
    )
    period = jnp.left_shift(jnp.ones((baselines, 1), jnp.int32), at_all[:, time_at : time_at + 1])
    begin = me - (me & (period - 1))
    lane = iota((baselines, LANES), 1)
    tile = jnp.sum(
        jnp.where(lane == begin, table[...], 0.0), axis=1, keepdims=True
    ).astype(jnp.int32)
    tile = tile + n_tiles * at_all[:, chan_at : chan_at + 1]
    n_share = (CLOG + 1) * n_tiles
    wide = -(-n_share // LANES) * LANES
    share = jnp.where(tile == iota((baselines, wide), 1), 1.0 / period.astype(F32), 0.0)
    share = share.T[:n_share].astype(BF16)

    def block_rows(k):
        at = pl.ds(pl.multiple_of(k * rows, rows), rows)
        return at, pl.ds(pl.multiple_of(baselines + k * rows, rows), rows)

    for other in across:
        gain_copy(0, other, other).wait_recv()
    chosen[0] = dot(pick, gains[0].reshape(n_chan * padded, 4 * width))

    def calibrate_early(k, carry):
        at, at_second = block_rows(k)
        coherency = as_matrix(split(send[k].astype(F32), width))
        partial = row_times(as_row(split(chosen[0, at, :], width)), coherency)
        partials[at, :] = flat(partial)
        entry = times_row_conj(partial, as_row(split(chosen[0, at_second, :], width)))
        calibrated[at, : 2 * width] = flat([entry]).astype(BF16)
        return carry

    lax.fori_loop(0, n_tm, calibrate_early, 0, unroll=2)
    early_send[...] = tile_sums(share, calibrated[:, : 2 * width], stacked, n_tm, width)
    for other in around:
        start(tile_copy(0, other, me))
    early_tiles[me] = early_send[me]

    for other in across:
        gain_copy(1, other, other).wait_recv()
    chosen[1] = dot(pick, gains[1].reshape(n_chan * padded, 4 * width))

    def calibrate_late(k, carry):
        at, at_second = block_rows(k)
        coherency = as_matrix(split(send[k].astype(F32), width))
        upper = as_row(split(partials[at, :], width))
        lower = row_times(as_row(split(chosen[1, at, :], width)), coherency)
        right_upper = as_row(split(chosen[0, at_second, :], width))
        right_lower = as_row(split(chosen[1, at_second, :], width))
        entries = [
            times_row_conj(upper, right_lower),
            times_row_conj(lower, right_upper),
            times_row_conj(lower, right_lower),
        ]
        calibrated[at, 2 * width :] = flat(entries).astype(BF16)
        return carry

    lax.fori_loop(0, n_tm, calibrate_late, 0, unroll=2)
    late_send[...] = tile_sums(share, calibrated[:, 2 * width :], stacked, n_tm, width)
    for other in around:
        start(tile_copy(1, other, me))
    late_tiles[me] = late_send[me]

    for other in around:
        turn_copy(other, other).wait_recv()
    ends = (2 * baselines, 2 * baselines + rows, 2 * baselines + 2 * rows)
    left, right = [
        split(chosen[0, ends[j] : ends[j + 1], :], width)
        + split(chosen[1, ends[j] : ends[j + 1], :], width)
        for j in range(2)
    ]

    def calibrate_time(t, carry):
        result = jones_apply(left, split(turned[t].astype(F32), width), right)
        at = pl.ds(pl.multiple_of(t * rows, rows), rows)
        calibrated[at, :] = jnp.concatenate(result, axis=1).astype(BF16)
        return carry

    lax.fori_loop(0, n_tm, calibrate_time, 0, unroll=2)
    group = 2**TLOG
    time_level = jnp.broadcast_to(at_here[:, time_at : time_at + 1], (rows, width))
    chan_level = jnp.broadcast_to(at_here[:, chan_at : chan_at + 1], (rows, width))
    chan_level = jnp.concatenate([chan_level] * group, axis=0)
    for first in range(0, n_tm, group):
        at = slice(first * rows, (first + group) * rows)
        for i in range(8):
            part = channel_average(
                calibrated[at, i * width : (i + 1) * width], means, chan_level, width
            )
            current = [part[t * rows : (t + 1) * rows] for t in range(group)]
            result = list(current)
            for k in range(1, TLOG + 1):
                current = [
                    0.5 * (current[2 * j] + current[2 * j + 1]) for j in range(len(current) // 2)
                ]
                result = [
                    jnp.where(time_level >= k, current[t >> k], result[t]) for t in range(group)
                ]
            for t in range(group):
                avg_ref[first + t, i] = result[t].astype(BF16)

    for chunk in range(2):
        for other in around:
            tile_copy(chunk, other, other).wait_recv()
    for copy in copies:
        copy.wait_send()


def write_kernel(avg_ref, early_ref, late_ref, avg_hbm, grid_hbm, grid, done):
    averaged = pltpu.make_async_copy(avg_ref, avg_hbm, done.at[0])
    averaged.start()
    tile_rows = grid.shape[0]
    first = 0
    for ref in (early_ref, late_ref):
        total = ref[0].astype(F32)
        for m in range(1, ref.shape[0]):
            total = total + ref[m].astype(F32)
        count = ref.shape[1] // tile_rows
        for i in range(count):
            grid[:, first + i, :] = total[i * tile_rows : (i + 1) * tile_rows]
        first += count
    gridded = pltpu.make_async_copy(grid, grid_hbm, done.at[1])
    gridded.start()
    averaged.wait()
    gridded.wait()


def shards(n_tm, n_chan, tile_count, visibilities, station_gains, station_pairs, average_bands, tile_map, baseline_order):
    baselines, width = visibilities.shape[2:]
    rows = baselines // n_tm
    stations = station_gains.shape[1]
    padded = -(-stations // 16) * 16
    tile_rows = tile_count // n_tm
    vmem = pl.BlockSpec(memory_space=pltpu.VMEM)
    dma = pltpu.SemaphoreType.DMA
    hbm = functools.partial(pltpu.with_memory_space_constraint, memory_space=pltpu.HBM)
    near = functools.partial(pltpu.with_memory_space_constraint, memory_space=pltpu.VMEM)
    averaged, early, late = pl.pallas_call(
        functools.partial(kernel, n_tm, n_chan),
        out_shape=(
            pltpu.VMEM((n_tm, 8, rows, width), BF16),
            pltpu.VMEM((n_tm, 2 * tile_rows, width), BF16),
            pltpu.VMEM((n_tm, 6 * tile_rows, width), BF16),
        ),
        in_specs=[pl.BlockSpec(memory_space=pl.ANY)] * 6,
        out_specs=(vmem,) * 3,
        scratch_shapes=[
            pltpu.VMEM((8, baselines, width), BF16),
            pltpu.VMEM(station_gains.shape, F32),
            pltpu.VMEM((2, baselines), jnp.int32),
            pltpu.VMEM((2, baselines), jnp.int32),
            pltpu.VMEM((n_tm, baselines), jnp.int32),
            pltpu.VMEM((1, baselines), jnp.int32),
            dma((7,)),
            pltpu.VMEM((LANES, baselines), F32),
            pltpu.VMEM((n_tm, rows, 8 * width), BF16),
            pltpu.VMEM((n_tm, rows, 8 * width), BF16),
            pltpu.VMEM((2, n_chan, padded, 4 * width), BF16),
            pltpu.VMEM((2, n_chan, padded, 4 * width), BF16),
            pltpu.VMEM((baselines, LANES), F32),
            pltpu.VMEM((2, 2 * baselines + 2 * rows, 4 * width), F32),
            pltpu.VMEM((baselines, 4 * width), F32),
            pltpu.VMEM((baselines, 8 * width), BF16),
            pltpu.VMEM((n_tm, 2 * tile_rows, width), BF16),
            pltpu.VMEM((n_tm, 6 * tile_rows, width), BF16),
            dma((n_tm,)),
            dma((n_tm,)),
            dma((2, n_chan)),
            dma((2, n_chan)),
            dma((2, n_tm)),
            dma((2, n_tm)),
        ],
        compiler_params=pltpu.CompilerParams(
            collective_id=0, has_side_effects=True, vmem_limit_bytes=40 * 2**20
        ),
        cost_estimate=pl.CostEstimate(
            flops=2 * 10**8, bytes_accessed=2 * 10**6, transcendentals=0
        ),
    )(
        hbm(visibilities),
        hbm(station_gains),
        hbm(station_pairs.T),
        hbm(average_bands.T),
        hbm(tile_map.T),
        hbm(baseline_order.reshape(1, baselines)),
    )
    return pl.pallas_call(
        write_kernel,
        out_shape=(
            pltpu.HBM(averaged.shape, BF16),
            pltpu.HBM((tile_rows, 8, width), F32),
        ),
        in_specs=[vmem] * 3,
        out_specs=(pl.BlockSpec(memory_space=pltpu.HBM),) * 2,
        scratch_shapes=[pltpu.VMEM((tile_rows, 8, width), F32), dma((2,))],
        compiler_params=pltpu.CompilerParams(vmem_limit_bytes=8 * 2**20),
        cost_estimate=pl.CostEstimate(flops=10**6, bytes_accessed=10**6, transcendentals=0),
    )(near(averaged), near(early), near(late))


def solution(mesh):
    n_tm, n_chan = mesh.shape["tm"], mesh.shape["chan"]
    tile_count = 8 * n_tm
    return jax.shard_map(
        functools.partial(shards, n_tm, n_chan, tile_count),
        mesh=mesh,
        in_specs=(P("tm", None, None, "chan"), P(None, "chan", None), P(), P(), P(), P()),
        out_specs=(P(None, None, "tm", "chan"), P("tm", None, "chan")),
        check_vma=False,
    )
```

```python
import functools

import jax
import jax.numpy as jnp
from jax import lax
from jax.experimental import pallas as pl
from jax.experimental.pallas import tpu as pltpu
from jax.sharding import PartitionSpec as P

TLOG = 3
CLOG = 2
TILE_BITS = 3
LANES = 128
MESH = pl.DeviceIdType.MESH
F32 = jnp.float32
BF16 = jnp.bfloat16


def product(left, right):
    return (left[0] * right[0] - left[1] * right[1], left[0] * right[1] + left[1] * right[0])


def product_conj(left, right):
    return (left[0] * right[0] + left[1] * right[1], left[1] * right[0] - left[0] * right[1])


def add_pair(left, right):
    return (left[0] + right[0], left[1] + right[1])


def as_matrix(components):
    return [
        [(components[0], components[1]), (components[2], components[3])],
        [(components[4], components[5]), (components[6], components[7])],
    ]


def jones_apply(first, middle, second):
    left_gain = as_matrix(first)
    coherency = as_matrix(middle)
    right_gain = as_matrix(second)
    partial_rows = [
        [
            add_pair(
                product(left_gain[i][0], coherency[0][k]), product(left_gain[i][1], coherency[1][k])
            )
            for k in range(2)
        ]
        for i in range(2)
    ]
    result = []
    for i in range(2):
        for c in range(2):
            element = add_pair(
                product_conj(partial_rows[i][0], right_gain[c][0]),
                product_conj(partial_rows[i][1], right_gain[c][1]),
            )
            result.extend(element)
    return result


def split(values, width):
    return [values[:, i * width : (i + 1) * width] for i in range(values.shape[1] // width)]


def iota(shape, axis):
    return lax.broadcasted_iota(jnp.int32, shape, axis)


def dot(left, right):
    return jnp.dot(left, right, preferred_element_type=F32)


def one_hot(column, ids):
    return jnp.where(column == ids, 1.0, 0.0).astype(BF16)


def channel_means(width):
    row = iota((width, width), 0)
    column = iota((width, width), 1)
    means = []
    for level in range(1, CLOG + 1):
        same = (row >> level) == (column >> level)
        means.append(jnp.where(same, 2.0**-level, 0.0))
    return jnp.concatenate(means, axis=1).astype(BF16)


def row_times(row, middle):
    return [
        add_pair(product(row[0], middle[0][b]), product(row[1], middle[1][b])) for b in range(2)
    ]


def times_row_conj(partial, row):
    return add_pair(product_conj(partial[0], row[0]), product_conj(partial[1], row[1]))


def as_row(components):
    return [(components[0], components[1]), (components[2], components[3])]


def flat(pairs):
    return jnp.concatenate([part for pair in pairs for part in pair], axis=1)


def tile_sums(share, samples, means, blocks, width):
    count = samples.shape[1] // width
    summed = dot(share, samples)
    n_tiles = share.shape[0] // (CLOG + 1)
    levels = []
    for i in range(count):
        part = summed[:, i * width : (i + 1) * width]
        levels.append(
            jnp.concatenate(
                [part[k * n_tiles : (k + 1) * n_tiles] for k in range(1, CLOG + 1)], axis=1
            )
        )
    spread = dot(jnp.concatenate(levels, axis=0).astype(BF16), means)
    result = []
    for i in range(count):
        part = summed[:n_tiles, i * width : (i + 1) * width]
        part = part + spread[i * n_tiles : (i + 1) * n_tiles]
        result.append(part.reshape(blocks, n_tiles // blocks, width))
    return jnp.concatenate(result, axis=1).astype(BF16)


def channel_average(samples, means, level, width):
    averaged = dot(samples, means)
    result = samples.astype(F32)
    for k in range(1, CLOG + 1):
        result = jnp.where(level >= k, averaged[:, (k - 1) * width : k * width], result)
    return result


def peers(mine, count):
    chips = count // 2
    chip = mine // 2
    core = lax.rem(mine, 2)
    others = []
    for step in range(1, chips):
        for flip in range(2):
            others.append(lax.rem(chip + step, chips) * 2 + lax.rem(core + flip, 2))
    return others + [chip * 2 + 1 - core]


def kernel(
    n_tm, n_chan,
    vis_hbm, gain_hbm, pairs_hbm, bands_hbm, map_hbm, order_hbm, avg_ref, early_tiles, late_tiles,
    vis_ref, gain_ref, pairs_ref, bands_ref, map_ref, order_ref, local, index,
    send, turned, gain_send, gains, table, chosen, partials, calibrated,
    early_send, late_send, early_pair, late_pair, early_sum, late_sum,
    turn_out, turn_in, gain_out, gain_in, tile_out, tile_in, pair_out, pair_in,
):
    me = lax.axis_index("tm")
    mine = lax.axis_index("chan")
    baselines = vis_ref.shape[1]
    width = vis_ref.shape[2]
    rows = baselines // n_tm
    stations = gain_ref.shape[1]
    padded = gain_send.shape[2]
    tile_rows = early_tiles.shape[1] // 2
    n_tiles = tile_rows * n_tm
    times = map_ref.shape[0]
    first_at, second_at, time_at, chan_at = range(times, times + 4)
    around = [step + lax.div(step - me + n_tm, n_tm) for step in range(n_tm - 1)]
    across = peers(mine, n_chan)
    half = n_tm // 2
    line = lax.rem(me, 2)
    spot = lax.div(me, 2)
    spots = [lax.rem(spot + step, half) for step in range(1, half)]

    sources = (
        gain_hbm.at[0:4], order_hbm, gain_hbm.at[4:8], vis_hbm.at[0], pairs_hbm, bands_hbm, map_hbm
    )
    targets = (
        gain_ref.at[0:4], order_ref, gain_ref.at[4:8], vis_ref, pairs_ref, bands_ref, map_ref
    )
    loads = [
        pltpu.make_async_copy(source, target, local.at[i])
        for i, (source, target) in enumerate(zip(sources, targets))
    ]
    for load in loads:
        load.start()

    barrier = pltpu.get_barrier_semaphore()
    for other in around:
        pl.semaphore_signal(barrier, inc=1, device_id={"tm": other}, device_id_type=MESH)
    for other in across:
        pl.semaphore_signal(barrier, inc=1, device_id={"chan": other}, device_id_type=MESH)

    def pack_gains(half):
        for c in range(n_chan):
            block = jnp.concatenate(
                [
                    gain_ref[4 * half + i, :, c * width : (c + 1) * width] for i in range(4)
                ],
                axis=1,
            )
            if padded > stations:
                block = jnp.concatenate(
                    [block, jnp.zeros((padded - stations, 4 * width), F32)], axis=0
                )
            gain_send[half, c] = block.astype(BF16)

    def gain_copy(half, other, slot):
        return pltpu.make_async_remote_copy(
            src_ref=gain_send.at[half, other],
            dst_ref=gains.at[half, slot],
            send_sem=gain_out.at[half, other],
            recv_sem=gain_in.at[half, slot],
            device_id={"chan": other},
            device_id_type=MESH,
        )

    def turn_copy(other, slot):
        return pltpu.make_async_remote_copy(
            src_ref=send.at[other],
            dst_ref=turned.at[slot],
            send_sem=turn_out.at[other],
            recv_sem=turn_in.at[slot],
            device_id={"tm": other},
            device_id_type=MESH,
        )

    chunks = (
        (early_send, early_pair, early_sum, early_tiles),
        (late_send, late_pair, late_sum, late_tiles),
    )

    def pair_copy(chunk):
        source, target = chunks[chunk][:2]
        return pltpu.make_async_remote_copy(
            src_ref=source.at[pl.ds((1 - line) * half, half)],
            dst_ref=target,
            send_sem=pair_out.at[chunk],
            recv_sem=pair_in.at[chunk],
            device_id={"tm": spot * 2 + 1 - line},
            device_id_type=MESH,
        )

    def tile_copy(chunk, other, slot):
        source, target = chunks[chunk][2:]
        return pltpu.make_async_remote_copy(
            src_ref=source.at[other],
            dst_ref=target.at[slot],
            send_sem=tile_out.at[chunk, other],
            recv_sem=tile_in.at[chunk, slot],
            device_id={"tm": other * 2 + line},
            device_id_type=MESH,
        )

    def pass_on(chunk):
        own, pair, both, target = chunks[chunk]
        pair_copy(chunk).wait_recv()
        total = own[pl.ds(line * half, half)].astype(F32) + pair[...].astype(F32)
        both[...] = total.astype(BF16)
        for other in spots:
            start(tile_copy(chunk, other, spot))
        target[spot] = both[spot]

    copies = []

    def start(copy):
        copy.start()
        copies.append(copy)

    loads[0].wait()
    pack_gains(0)
    loads[1].wait()
    place = jnp.where(order_ref[...] == iota((baselines, baselines), 0), 1.0, 0.0)
    place = place.T.astype(BF16)

    pl.semaphore_wait(barrier, n_tm + n_chan - 2)

    for other in across:
        start(gain_copy(0, other, mine))
    loads[2].wait()
    pack_gains(1)
    for other in across:
        start(gain_copy(1, other, mine))

    loads[3].wait()
    raw = jnp.concatenate([vis_ref[i] for i in range(8)], axis=1)
    send[...] = dot(place, raw).astype(BF16).reshape(send.shape)
    for other in around:
        start(turn_copy(other, me))

    turned[me] = send[me]
    gains[0, mine] = gain_send[0, mine]
    gains[1, mine] = gain_send[1, mine]
    means = channel_means(width)
    stacked = jnp.concatenate(
        [means[:, k * width : (k + 1) * width] for k in range(CLOG)], axis=0
    )
    for load in loads[4:]:
        load.wait()
    index[...] = jnp.zeros_like(index)
    index[:times] = map_ref[...].astype(F32)
    index[first_at : second_at + 1] = pairs_ref[...].astype(F32)
    index[time_at : chan_at + 1] = bands_ref[...].astype(F32)
    table[...] = lax.dot_general(
        place, index[...].astype(BF16), (((1,), (1,)), ((), ())), preferred_element_type=F32
    )

    ids = iota((1, n_chan * padded), 1)
    if padded > stations:
        lane = ids
        for c in range(n_chan):
            inside = (lane >= c * padded) & (lane < c * padded + stations)
            ids = jnp.where(inside, lane - c * (padded - stations), ids)
            ids = jnp.where((lane >= c * padded + stations) & (lane < (c + 1) * padded), -1, ids)
    here = pl.ds(pl.multiple_of(me * rows, rows), rows)
    at_all = table[...].astype(jnp.int32)
    at_here = table[here, :].astype(jnp.int32)
    pick = jnp.concatenate(
        [
            one_hot(at_all[:, first_at : first_at + 1], ids),
            one_hot(at_all[:, second_at : second_at + 1], ids),
            one_hot(at_here[:, first_at : first_at + 1], ids),
            one_hot(at_here[:, second_at : second_at + 1], ids),
        ],
        axis=0,
    )
    period = jnp.left_shift(jnp.ones((baselines, 1), jnp.int32), at_all[:, time_at : time_at + 1])
    begin = me - (me & (period - 1))
    lane = iota((baselines, LANES), 1)
    tile = jnp.sum(
        jnp.where(lane == begin, table[...], 0.0), axis=1, keepdims=True
    ).astype(jnp.int32)
    owner = tile >> TILE_BITS
    tile = (((owner & 1) * half + (owner >> 1)) << TILE_BITS) + (tile & (tile_rows - 1))
    tile = tile + n_tiles * at_all[:, chan_at : chan_at + 1]
    n_share = (CLOG + 1) * n_tiles
    wide = -(-n_share // LANES) * LANES
    share = jnp.where(tile == iota((baselines, wide), 1), 1.0 / period.astype(F32), 0.0)
    share = share.T[:n_share].astype(BF16)

    def block_rows(k):
        at = pl.ds(pl.multiple_of(k * rows, rows), rows)
        return at, pl.ds(pl.multiple_of(baselines + k * rows, rows), rows)

    for other in across:
        gain_copy(0, other, other).wait_recv()
    chosen[0] = dot(pick, gains[0].reshape(n_chan * padded, 4 * width))

    def calibrate_early(k, carry):
        at, at_second = block_rows(k)
        coherency = as_matrix(split(send[k].astype(F32), width))
        partial = row_times(as_row(split(chosen[0, at, :], width)), coherency)
        partials[at, :] = flat(partial)
        entry = times_row_conj(partial, as_row(split(chosen[0, at_second, :], width)))
        calibrated[at, : 2 * width] = flat([entry]).astype(BF16)
        return carry

    lax.fori_loop(0, n_tm, calibrate_early, 0, unroll=2)
    early_send[...] = tile_sums(share, calibrated[:, : 2 * width], stacked, n_tm, width)
    start(pair_copy(0))

    for other in across:
        gain_copy(1, other, other).wait_recv()
    chosen[1] = dot(pick, gains[1].reshape(n_chan * padded, 4 * width))

    def calibrate_late(k, carry):
        at, at_second = block_rows(k)
        coherency = as_matrix(split(send[k].astype(F32), width))
        upper = as_row(split(partials[at, :], width))
        lower = row_times(as_row(split(chosen[1, at, :], width)), coherency)
        right_upper = as_row(split(chosen[0, at_second, :], width))
        right_lower = as_row(split(chosen[1, at_second, :], width))
        entries = [
            times_row_conj(upper, right_lower),
            times_row_conj(lower, right_upper),
            times_row_conj(lower, right_lower),
        ]
        calibrated[at, 2 * width :] = flat(entries).astype(BF16)
        return carry

    lax.fori_loop(0, n_tm, calibrate_late, 0, unroll=2)
    pass_on(0)
    late_send[...] = tile_sums(share, calibrated[:, 2 * width :], stacked, n_tm, width)
    start(pair_copy(1))
    pass_on(1)

    for other in around:
        turn_copy(other, other).wait_recv()
    ends = (2 * baselines, 2 * baselines + rows, 2 * baselines + 2 * rows)
    left, right = [
        split(chosen[0, ends[j] : ends[j + 1], :], width)
        + split(chosen[1, ends[j] : ends[j + 1], :], width)
        for j in range(2)
    ]

    def calibrate_time(t, carry):
        result = jones_apply(left, split(turned[t].astype(F32), width), right)
        at = pl.ds(pl.multiple_of(t * rows, rows), rows)
        calibrated[at, :] = jnp.concatenate(result, axis=1).astype(BF16)
        return carry

    lax.fori_loop(0, n_tm, calibrate_time, 0, unroll=2)
    group = 2**TLOG
    time_level = jnp.broadcast_to(at_here[:, time_at : time_at + 1], (rows, width))
    chan_level = jnp.broadcast_to(at_here[:, chan_at : chan_at + 1], (rows, width))
    chan_level = jnp.concatenate([chan_level] * group, axis=0)
    for first in range(0, n_tm, group):
        at = slice(first * rows, (first + group) * rows)
        for i in range(8):
            part = channel_average(
                calibrated[at, i * width : (i + 1) * width], means, chan_level, width
            )
            current = [part[t * rows : (t + 1) * rows] for t in range(group)]
            result = list(current)
            for k in range(1, TLOG + 1):
                current = [
                    0.5 * (current[2 * j] + current[2 * j + 1]) for j in range(len(current) // 2)
                ]
                result = [
                    jnp.where(time_level >= k, current[t >> k], result[t]) for t in range(group)
                ]
            for t in range(group):
                avg_ref[first + t, i] = result[t].astype(BF16)

    for chunk in range(2):
        for other in spots:
            tile_copy(chunk, other, other).wait_recv()
    for copy in copies:
        copy.wait_send()


def write_kernel(avg_ref, early_ref, late_ref, avg_hbm, grid_hbm, grid, done):
    averaged = pltpu.make_async_copy(avg_ref, avg_hbm, done.at[0])
    averaged.start()
    tile_rows = grid.shape[0]
    first = 0
    for ref in (early_ref, late_ref):
        total = ref[0].astype(F32)
        for m in range(1, ref.shape[0]):
            total = total + ref[m].astype(F32)
        count = ref.shape[1] // tile_rows
        for i in range(count):
            grid[:, first + i, :] = total[i * tile_rows : (i + 1) * tile_rows]
        first += count
    gridded = pltpu.make_async_copy(grid, grid_hbm, done.at[1])
    gridded.start()
    averaged.wait()
    gridded.wait()


def shards(n_tm, n_chan, tile_count, visibilities, station_gains, station_pairs, average_bands, tile_map, baseline_order):
    baselines, width = visibilities.shape[2:]
    rows = baselines // n_tm
    stations = station_gains.shape[1]
    padded = -(-stations // 16) * 16
    tile_rows = tile_count // n_tm
    vmem = pl.BlockSpec(memory_space=pltpu.VMEM)
    dma = pltpu.SemaphoreType.DMA
    hbm = functools.partial(pltpu.with_memory_space_constraint, memory_space=pltpu.HBM)
    near = functools.partial(pltpu.with_memory_space_constraint, memory_space=pltpu.VMEM)
    averaged, early, late = pl.pallas_call(
        functools.partial(kernel, n_tm, n_chan),
        out_shape=(
            pltpu.VMEM((n_tm, 8, rows, width), BF16),
            pltpu.VMEM((n_tm // 2, 2 * tile_rows, width), BF16),
            pltpu.VMEM((n_tm // 2, 6 * tile_rows, width), BF16),
        ),
        in_specs=[pl.BlockSpec(memory_space=pl.ANY)] * 6,
        out_specs=(vmem,) * 3,
        scratch_shapes=[
            pltpu.VMEM((8, baselines, width), BF16),
            pltpu.VMEM(station_gains.shape, F32),
            pltpu.VMEM((2, baselines), jnp.int32),
            pltpu.VMEM((2, baselines), jnp.int32),
            pltpu.VMEM((n_tm, baselines), jnp.int32),
            pltpu.VMEM((1, baselines), jnp.int32),
            dma((7,)),
            pltpu.VMEM((LANES, baselines), F32),
            pltpu.VMEM((n_tm, rows, 8 * width), BF16),
            pltpu.VMEM((n_tm, rows, 8 * width), BF16),
            pltpu.VMEM((2, n_chan, padded, 4 * width), BF16),
            pltpu.VMEM((2, n_chan, padded, 4 * width), BF16),
            pltpu.VMEM((baselines, LANES), F32),
            pltpu.VMEM((2, 2 * baselines + 2 * rows, 4 * width), F32),
            pltpu.VMEM((baselines, 4 * width), F32),
            pltpu.VMEM((baselines, 8 * width), BF16),
            pltpu.VMEM((n_tm, 2 * tile_rows, width), BF16),
            pltpu.VMEM((n_tm, 6 * tile_rows, width), BF16),
            pltpu.VMEM((n_tm // 2, 2 * tile_rows, width), BF16),
            pltpu.VMEM((n_tm // 2, 6 * tile_rows, width), BF16),
            pltpu.VMEM((n_tm // 2, 2 * tile_rows, width), BF16),
            pltpu.VMEM((n_tm // 2, 6 * tile_rows, width), BF16),
            dma((n_tm,)),
            dma((n_tm,)),
            dma((2, n_chan)),
            dma((2, n_chan)),
            dma((2, n_tm // 2)),
            dma((2, n_tm // 2)),
            dma((2,)),
            dma((2,)),
        ],
        compiler_params=pltpu.CompilerParams(
            collective_id=0, has_side_effects=True, vmem_limit_bytes=40 * 2**20
        ),
        cost_estimate=pl.CostEstimate(
            flops=2 * 10**8, bytes_accessed=2 * 10**6, transcendentals=0
        ),
    )(
        hbm(visibilities),
        hbm(station_gains),
        hbm(station_pairs.T),
        hbm(average_bands.T),
        hbm(tile_map.T),
        hbm(baseline_order.reshape(1, baselines)),
    )
    return pl.pallas_call(
        write_kernel,
        out_shape=(
            pltpu.HBM(averaged.shape, BF16),
            pltpu.HBM((tile_rows, 8, width), F32),
        ),
        in_specs=[vmem] * 3,
        out_specs=(pl.BlockSpec(memory_space=pltpu.HBM),) * 2,
        scratch_shapes=[pltpu.VMEM((tile_rows, 8, width), F32), dma((2,))],
        compiler_params=pltpu.CompilerParams(vmem_limit_bytes=8 * 2**20),
        cost_estimate=pl.CostEstimate(flops=10**6, bytes_accessed=10**6, transcendentals=0),
    )(near(averaged), near(early), near(late))


def solution(mesh):
    n_tm, n_chan = mesh.shape["tm"], mesh.shape["chan"]
    tile_count = n_tm << TILE_BITS
    return jax.shard_map(
        functools.partial(shards, n_tm, n_chan, tile_count),
        mesh=mesh,
        in_specs=(P("tm", None, None, "chan"), P(None, "chan", None), P(), P(), P(), P()),
        out_specs=(P(None, None, "tm", "chan"), P("tm", None, "chan")),
        check_vma=False,
    )
```

```python
import functools

import jax
import jax.numpy as jnp
from jax import lax
from jax.experimental import pallas as pl
from jax.experimental.pallas import tpu as pltpu
from jax.sharding import PartitionSpec as P

TLOG = 3
CLOG = 2
LANES = 128
MESH = pl.DeviceIdType.MESH
F32 = jnp.float32
BF16 = jnp.bfloat16


def product(left, right):
    return (left[0] * right[0] - left[1] * right[1], left[0] * right[1] + left[1] * right[0])


def product_conj(left, right):
    return (left[0] * right[0] + left[1] * right[1], left[1] * right[0] - left[0] * right[1])


def add_pair(left, right):
    return (left[0] + right[0], left[1] + right[1])


def as_matrix(components):
    return [
        [(components[0], components[1]), (components[2], components[3])],
        [(components[4], components[5]), (components[6], components[7])],
    ]


def jones_apply(first, middle, second):
    left_gain = as_matrix(first)
    coherency = as_matrix(middle)
    right_gain = as_matrix(second)
    partial_rows = [
        [
            add_pair(
                product(left_gain[i][0], coherency[0][k]), product(left_gain[i][1], coherency[1][k])
            )
            for k in range(2)
        ]
        for i in range(2)
    ]
    result = []
    for i in range(2):
        for c in range(2):
            element = add_pair(
                product_conj(partial_rows[i][0], right_gain[c][0]),
                product_conj(partial_rows[i][1], right_gain[c][1]),
            )
            result.extend(element)
    return result


def split(values, width):
    return [values[:, i * width : (i + 1) * width] for i in range(values.shape[1] // width)]


def iota(shape, axis):
    return lax.broadcasted_iota(jnp.int32, shape, axis)


def dot(left, right):
    return jnp.dot(left, right, preferred_element_type=F32)


def one_hot(column, ids):
    return jnp.where(column == ids, 1.0, 0.0).astype(BF16)


def channel_means(width):
    row = iota((width, width), 0)
    column = iota((width, width), 1)
    means = []
    for level in range(1, CLOG + 1):
        same = (row >> level) == (column >> level)
        means.append(jnp.where(same, 2.0**-level, 0.0))
    return jnp.concatenate(means, axis=1).astype(BF16)


def row_times(row, middle):
    return [
        add_pair(product(row[0], middle[0][b]), product(row[1], middle[1][b])) for b in range(2)
    ]


def times_row_conj(partial, row):
    return add_pair(product_conj(partial[0], row[0]), product_conj(partial[1], row[1]))


def as_row(components):
    return [(components[0], components[1]), (components[2], components[3])]


def flat(pairs):
    return jnp.concatenate([part for pair in pairs for part in pair], axis=1)


def tile_sums(share, samples, means, blocks, width):
    count = samples.shape[1] // width
    summed = dot(share, samples)
    n_tiles = share.shape[0] // (CLOG + 1)
    levels = []
    for i in range(count):
        part = summed[:, i * width : (i + 1) * width]
        levels.append(
            jnp.concatenate(
                [part[k * n_tiles : (k + 1) * n_tiles] for k in range(1, CLOG + 1)], axis=1
            )
        )
    spread = dot(jnp.concatenate(levels, axis=0).astype(BF16), means)
    result = []
    for i in range(count):
        part = summed[:n_tiles, i * width : (i + 1) * width]
        part = part + spread[i * n_tiles : (i + 1) * n_tiles]
        result.append(part.reshape(blocks, n_tiles // blocks, width))
    return jnp.concatenate(result, axis=1).astype(BF16)


def channel_average(samples, means, level, width):
    averaged = dot(samples, means)
    result = samples.astype(F32)
    for k in range(1, CLOG + 1):
        result = jnp.where(level >= k, averaged[:, (k - 1) * width : k * width], result)
    return result


def peers(mine, count):
    chips = count // 2
    chip = mine // 2
    core = lax.rem(mine, 2)
    others = []
    for step in range(1, chips):
        for flip in range(2):
            others.append(lax.rem(chip + step, chips) * 2 + lax.rem(core + flip, 2))
    return others + [chip * 2 + 1 - core]


def kernel(
    n_tm, n_chan,
    vis_hbm, gain_hbm, pairs_hbm, bands_hbm, map_hbm, order_hbm, avg_ref, early_tiles, late_tiles,
    vis_ref, gain_ref, pairs_ref, bands_ref, map_ref, order_ref, local, index,
    send, turned, gain_send, gains, table, chosen, partials, calibrated, early_send, late_send,
    turn_out, turn_in, gain_out, gain_in, tile_out, tile_in,
):
    me = lax.axis_index("tm")
    mine = lax.axis_index("chan")
    baselines = vis_ref.shape[1]
    width = vis_ref.shape[2]
    rows = baselines // n_tm
    stations = gain_ref.shape[1]
    padded = gain_send.shape[2]
    tile_rows = early_tiles.shape[1] // 2
    n_tiles = tile_rows * n_tm
    times = map_ref.shape[0]
    first_at, second_at, time_at, chan_at = range(times, times + 4)
    around = [step + lax.div(step - me + n_tm, n_tm) for step in range(n_tm - 1)]
    across = peers(mine, n_chan)

    sources = (
        gain_hbm.at[0:4], order_hbm, gain_hbm.at[4:8], vis_hbm.at[0], pairs_hbm, bands_hbm, map_hbm
    )
    targets = (
        gain_ref.at[0:4], order_ref, gain_ref.at[4:8], vis_ref, pairs_ref, bands_ref, map_ref
    )
    loads = [
        pltpu.make_async_copy(source, target, local.at[i])
        for i, (source, target) in enumerate(zip(sources, targets))
    ]
    for load in loads:
        load.start()

    barrier = pltpu.get_barrier_semaphore()
    for other in around:
        pl.semaphore_signal(barrier, inc=1, device_id={"tm": other}, device_id_type=MESH)
    for other in across:
        pl.semaphore_signal(barrier, inc=1, device_id={"chan": other}, device_id_type=MESH)

    def pack_gains(half):
        for c in range(n_chan):
            block = jnp.concatenate(
                [
                    gain_ref[4 * half + i, :, c * width : (c + 1) * width] for i in range(4)
                ],
                axis=1,
            )
            if padded > stations:
                block = jnp.concatenate(
                    [block, jnp.zeros((padded - stations, 4 * width), F32)], axis=0
                )
            gain_send[half, c] = block.astype(BF16)

    def gain_copy(half, other, slot):
        return pltpu.make_async_remote_copy(
            src_ref=gain_send.at[half, other],
            dst_ref=gains.at[half, slot],
            send_sem=gain_out.at[half, other],
            recv_sem=gain_in.at[half, slot],
            device_id={"chan": other},
            device_id_type=MESH,
        )

    def turn_copy(other, slot):
        return pltpu.make_async_remote_copy(
            src_ref=send.at[other],
            dst_ref=turned.at[slot],
            send_sem=turn_out.at[other],
            recv_sem=turn_in.at[slot],
            device_id={"tm": other},
            device_id_type=MESH,
        )

    def tile_copy(chunk, other, slot):
        source, target = ((early_send, early_tiles), (late_send, late_tiles))[chunk]
        return pltpu.make_async_remote_copy(
            src_ref=source.at[other],
            dst_ref=target.at[slot],
            send_sem=tile_out.at[chunk, other],
            recv_sem=tile_in.at[chunk, slot],
            device_id={"tm": other},
            device_id_type=MESH,
        )

    copies = []

    def start(copy):
        copy.start()
        copies.append(copy)

    loads[0].wait()
    pack_gains(0)
    loads[1].wait()
    place = jnp.where(order_ref[...] == iota((baselines, baselines), 0), 1.0, 0.0)
    place = place.T.astype(BF16)

    loads[3].wait()
    raw = jnp.concatenate([vis_ref[i] for i in range(8)], axis=1)
    send[...] = dot(place, raw).astype(BF16).reshape(send.shape)
    loads[2].wait()
    pack_gains(1)

    pl.semaphore_wait(barrier, n_tm + n_chan - 2)

    for other in across:
        start(gain_copy(0, other, mine))
    for other in around:
        start(turn_copy(other, me))
    for other in across:
        start(gain_copy(1, other, mine))

    turned[me] = send[me]
    gains[0, mine] = gain_send[0, mine]
    gains[1, mine] = gain_send[1, mine]
    means = channel_means(width)
    stacked = jnp.concatenate(
        [means[:, k * width : (k + 1) * width] for k in range(CLOG)], axis=0
    )
    for load in loads[4:]:
        load.wait()
    index[...] = jnp.zeros_like(index)
    index[:times] = map_ref[...].astype(F32)
    index[first_at : second_at + 1] = pairs_ref[...].astype(F32)
    index[time_at : chan_at + 1] = bands_ref[...].astype(F32)
    table[...] = lax.dot_general(
        place, index[...].astype(BF16), (((1,), (1,)), ((), ())), preferred_element_type=F32
    )

    ids = iota((1, n_chan * padded), 1)
    if padded > stations:
        lane = ids
        for c in range(n_chan):
            inside = (lane >= c * padded) & (lane < c * padded + stations)
            ids = jnp.where(inside, lane - c * (padded - stations), ids)
            ids = jnp.where((lane >= c * padded + stations) & (lane < (c + 1) * padded), -1, ids)
    here = pl.ds(pl.multiple_of(me * rows, rows), rows)
    at_all = table[...].astype(jnp.int32)
    at_here = table[here, :].astype(jnp.int32)
    pick = jnp.concatenate(
        [
            one_hot(at_all[:, first_at : first_at + 1], ids),
            one_hot(at_all[:, second_at : second_at + 1], ids),
            one_hot(at_here[:, first_at : first_at + 1], ids),
            one_hot(at_here[:, second_at : second_at + 1], ids),
        ],
        axis=0,
    )
    period = jnp.left_shift(jnp.ones((baselines, 1), jnp.int32), at_all[:, time_at : time_at + 1])
    begin = me - (me & (period - 1))
    lane = iota((baselines, LANES), 1)
    tile = jnp.sum(
        jnp.where(lane == begin, table[...], 0.0), axis=1, keepdims=True
    ).astype(jnp.int32)
    tile = tile + n_tiles * at_all[:, chan_at : chan_at + 1]
    n_share = (CLOG + 1) * n_tiles
    wide = -(-n_share // LANES) * LANES
    share = jnp.where(tile == iota((baselines, wide), 1), 1.0 / period.astype(F32), 0.0)
    share = share.T[:n_share].astype(BF16)

    def block_rows(k):
        at = pl.ds(pl.multiple_of(k * rows, rows), rows)
        return at, pl.ds(pl.multiple_of(baselines + k * rows, rows), rows)

    for other in across:
        gain_copy(0, other, other).wait_recv()
    chosen[0] = dot(pick, gains[0].reshape(n_chan * padded, 4 * width))

    def calibrate_early(k, carry):
        at, at_second = block_rows(k)
        coherency = as_matrix(split(send[k].astype(F32), width))
        partial = row_times(as_row(split(chosen[0, at, :], width)), coherency)
        partials[at, :] = flat(partial)
        entry = times_row_conj(partial, as_row(split(chosen[0, at_second, :], width)))
        calibrated[at, : 2 * width] = flat([entry]).astype(BF16)
        return carry

    lax.fori_loop(0, n_tm, calibrate_early, 0, unroll=2)
    early_send[...] = tile_sums(share, calibrated[:, : 2 * width], stacked, n_tm, width)
    for other in around:
        start(tile_copy(0, other, me))
    early_tiles[me] = early_send[me]

    for other in across:
        gain_copy(1, other, other).wait_recv()
    chosen[1] = dot(pick, gains[1].reshape(n_chan * padded, 4 * width))

    def calibrate_late(k, carry):
        at, at_second = block_rows(k)
        coherency = as_matrix(split(send[k].astype(F32), width))
        upper = as_row(split(partials[at, :], width))
        lower = row_times(as_row(split(chosen[1, at, :], width)), coherency)
        right_upper = as_row(split(chosen[0, at_second, :], width))
        right_lower = as_row(split(chosen[1, at_second, :], width))
        entries = [
            times_row_conj(upper, right_lower),
            times_row_conj(lower, right_upper),
            times_row_conj(lower, right_lower),
        ]
        calibrated[at, 2 * width :] = flat(entries).astype(BF16)
        return carry

    lax.fori_loop(0, n_tm, calibrate_late, 0, unroll=2)
    late_send[...] = tile_sums(share, calibrated[:, 2 * width :], stacked, n_tm, width)
    for other in around:
        start(tile_copy(1, other, me))
    late_tiles[me] = late_send[me]

    for other in around:
        turn_copy(other, other).wait_recv()
    ends = (2 * baselines, 2 * baselines + rows, 2 * baselines + 2 * rows)
    left, right = [
        split(chosen[0, ends[j] : ends[j + 1], :], width)
        + split(chosen[1, ends[j] : ends[j + 1], :], width)
        for j in range(2)
    ]

    def calibrate_time(t, carry):
        result = jones_apply(left, split(turned[t].astype(F32), width), right)
        at = pl.ds(pl.multiple_of(t * rows, rows), rows)
        calibrated[at, :] = jnp.concatenate(result, axis=1).astype(BF16)
        return carry

    lax.fori_loop(0, n_tm, calibrate_time, 0, unroll=2)
    group = 2**TLOG
    time_level = jnp.broadcast_to(at_here[:, time_at : time_at + 1], (rows, width))
    chan_level = jnp.broadcast_to(at_here[:, chan_at : chan_at + 1], (rows, width))
    chan_level = jnp.concatenate([chan_level] * group, axis=0)
    for first in range(0, n_tm, group):
        at = slice(first * rows, (first + group) * rows)
        for i in range(8):
            part = channel_average(
                calibrated[at, i * width : (i + 1) * width], means, chan_level, width
            )
            current = [part[t * rows : (t + 1) * rows] for t in range(group)]
            result = list(current)
            for k in range(1, TLOG + 1):
                current = [
                    0.5 * (current[2 * j] + current[2 * j + 1]) for j in range(len(current) // 2)
                ]
                result = [
                    jnp.where(time_level >= k, current[t >> k], result[t]) for t in range(group)
                ]
            for t in range(group):
                avg_ref[first + t, i] = result[t].astype(BF16)

    for chunk in range(2):
        for other in around:
            tile_copy(chunk, other, other).wait_recv()
    for copy in copies:
        copy.wait_send()


def write_kernel(avg_ref, early_ref, late_ref, avg_hbm, grid_hbm, grid, done):
    averaged = pltpu.make_async_copy(avg_ref, avg_hbm, done.at[0])
    averaged.start()
    tile_rows = grid.shape[0]
    first = 0
    for ref in (early_ref, late_ref):
        total = ref[0].astype(F32)
        for m in range(1, ref.shape[0]):
            total = total + ref[m].astype(F32)
        count = ref.shape[1] // tile_rows
        for i in range(count):
            grid[:, first + i, :] = total[i * tile_rows : (i + 1) * tile_rows]
        first += count
    gridded = pltpu.make_async_copy(grid, grid_hbm, done.at[1])
    gridded.start()
    averaged.wait()
    gridded.wait()


def shards(n_tm, n_chan, tile_count, visibilities, station_gains, station_pairs, average_bands, tile_map, baseline_order):
    baselines, width = visibilities.shape[2:]
    rows = baselines // n_tm
    stations = station_gains.shape[1]
    padded = -(-stations // 16) * 16
    tile_rows = tile_count // n_tm
    vmem = pl.BlockSpec(memory_space=pltpu.VMEM)
    dma = pltpu.SemaphoreType.DMA
    hbm = functools.partial(pltpu.with_memory_space_constraint, memory_space=pltpu.HBM)
    near = functools.partial(pltpu.with_memory_space_constraint, memory_space=pltpu.VMEM)
    averaged, early, late = pl.pallas_call(
        functools.partial(kernel, n_tm, n_chan),
        out_shape=(
            pltpu.VMEM((n_tm, 8, rows, width), BF16),
            pltpu.VMEM((n_tm, 2 * tile_rows, width), BF16),
            pltpu.VMEM((n_tm, 6 * tile_rows, width), BF16),
        ),
        in_specs=[pl.BlockSpec(memory_space=pl.ANY)] * 6,
        out_specs=(vmem,) * 3,
        scratch_shapes=[
            pltpu.VMEM((8, baselines, width), BF16),
            pltpu.VMEM(station_gains.shape, F32),
            pltpu.VMEM((2, baselines), jnp.int32),
            pltpu.VMEM((2, baselines), jnp.int32),
            pltpu.VMEM((n_tm, baselines), jnp.int32),
            pltpu.VMEM((1, baselines), jnp.int32),
            dma((7,)),
            pltpu.VMEM((LANES, baselines), F32),
            pltpu.VMEM((n_tm, rows, 8 * width), BF16),
            pltpu.VMEM((n_tm, rows, 8 * width), BF16),
            pltpu.VMEM((2, n_chan, padded, 4 * width), BF16),
            pltpu.VMEM((2, n_chan, padded, 4 * width), BF16),
            pltpu.VMEM((baselines, LANES), F32),
            pltpu.VMEM((2, 2 * baselines + 2 * rows, 4 * width), F32),
            pltpu.VMEM((baselines, 4 * width), F32),
            pltpu.VMEM((baselines, 8 * width), BF16),
            pltpu.VMEM((n_tm, 2 * tile_rows, width), BF16),
            pltpu.VMEM((n_tm, 6 * tile_rows, width), BF16),
            dma((n_tm,)),
            dma((n_tm,)),
            dma((2, n_chan)),
            dma((2, n_chan)),
            dma((2, n_tm)),
            dma((2, n_tm)),
        ],
        compiler_params=pltpu.CompilerParams(
            collective_id=0, has_side_effects=True, vmem_limit_bytes=40 * 2**20
        ),
        cost_estimate=pl.CostEstimate(
            flops=2 * 10**8, bytes_accessed=2 * 10**6, transcendentals=0
        ),
    )(
        hbm(visibilities),
        hbm(station_gains),
        hbm(station_pairs.T),
        hbm(average_bands.T),
        hbm(tile_map.T),
        hbm(baseline_order.reshape(1, baselines)),
    )
    return pl.pallas_call(
        write_kernel,
        out_shape=(
            pltpu.HBM(averaged.shape, BF16),
            pltpu.HBM((tile_rows, 8, width), F32),
        ),
        in_specs=[vmem] * 3,
        out_specs=(pl.BlockSpec(memory_space=pltpu.HBM),) * 2,
        scratch_shapes=[pltpu.VMEM((tile_rows, 8, width), F32), dma((2,))],
        compiler_params=pltpu.CompilerParams(vmem_limit_bytes=8 * 2**20),
        cost_estimate=pl.CostEstimate(flops=10**6, bytes_accessed=10**6, transcendentals=0),
    )(near(averaged), near(early), near(late))


def solution(mesh):
    n_tm, n_chan = mesh.shape["tm"], mesh.shape["chan"]
    tile_count = 8 * n_tm
    return jax.shard_map(
        functools.partial(shards, n_tm, n_chan, tile_count),
        mesh=mesh,
        in_specs=(P("tm", None, None, "chan"), P(None, "chan", None), P(), P(), P(), P()),
        out_specs=(P(None, None, "tm", "chan"), P("tm", None, "chan")),
        check_vma=False,
    )
```

```python
import functools

import jax
import jax.numpy as jnp
from jax import lax
from jax.experimental import pallas as pl
from jax.experimental.pallas import tpu as pltpu
from jax.sharding import PartitionSpec as P

TLOG = 3
CLOG = 2
LANES = 128
MESH = pl.DeviceIdType.MESH
F32 = jnp.float32
BF16 = jnp.bfloat16


def product(left, right):
    return (left[0] * right[0] - left[1] * right[1], left[0] * right[1] + left[1] * right[0])


def product_conj(left, right):
    return (left[0] * right[0] + left[1] * right[1], left[1] * right[0] - left[0] * right[1])


def add_pair(left, right):
    return (left[0] + right[0], left[1] + right[1])


def as_matrix(components):
    return [
        [(components[0], components[1]), (components[2], components[3])],
        [(components[4], components[5]), (components[6], components[7])],
    ]


def jones_apply(first, middle, second):
    left_gain = as_matrix(first)
    coherency = as_matrix(middle)
    right_gain = as_matrix(second)
    partial_rows = [
        [
            add_pair(
                product(left_gain[i][0], coherency[0][k]), product(left_gain[i][1], coherency[1][k])
            )
            for k in range(2)
        ]
        for i in range(2)
    ]
    result = []
    for i in range(2):
        for c in range(2):
            element = add_pair(
                product_conj(partial_rows[i][0], right_gain[c][0]),
                product_conj(partial_rows[i][1], right_gain[c][1]),
            )
            result.extend(element)
    return result


def split(values, width):
    return [values[:, i * width : (i + 1) * width] for i in range(values.shape[1] // width)]


def iota(shape, axis):
    return lax.broadcasted_iota(jnp.int32, shape, axis)


def dot(left, right):
    return jnp.dot(left, right, preferred_element_type=F32)


def one_hot(column, ids):
    return jnp.where(column == ids, 1.0, 0.0).astype(BF16)


def channel_means(width):
    row = iota((width, width), 0)
    column = iota((width, width), 1)
    means = []
    for level in range(1, CLOG + 1):
        same = (row >> level) == (column >> level)
        means.append(jnp.where(same, 2.0**-level, 0.0))
    return jnp.concatenate(means, axis=1).astype(BF16)


def row_times(row, middle):
    return [
        add_pair(product(row[0], middle[0][b]), product(row[1], middle[1][b])) for b in range(2)
    ]


def times_row_conj(partial, row):
    return add_pair(product_conj(partial[0], row[0]), product_conj(partial[1], row[1]))


def as_row(components):
    return [(components[0], components[1]), (components[2], components[3])]


def flat(pairs):
    return jnp.concatenate([part for pair in pairs for part in pair], axis=1)


def tile_sums(share, samples, means, blocks, width):
    count = samples.shape[1] // width
    summed = dot(share, samples)
    n_tiles = share.shape[0] // (CLOG + 1)
    levels = []
    for i in range(count):
        part = summed[:, i * width : (i + 1) * width]
        levels.append(
            jnp.concatenate(
                [part[k * n_tiles : (k + 1) * n_tiles] for k in range(1, CLOG + 1)], axis=1
            )
        )
    spread = dot(jnp.concatenate(levels, axis=0).astype(BF16), means)
    result = []
    for i in range(count):
        part = summed[:n_tiles, i * width : (i + 1) * width]
        part = part + spread[i * n_tiles : (i + 1) * n_tiles]
        result.append(part.reshape(blocks, n_tiles // blocks, width))
    return jnp.concatenate(result, axis=1).astype(BF16)


def channel_average(samples, means, level, width):
    averaged = dot(samples, means)
    result = samples.astype(F32)
    for k in range(1, CLOG + 1):
        result = jnp.where(level >= k, averaged[:, (k - 1) * width : k * width], result)
    return result


def peers(mine, count):
    chips = count // 2
    chip = mine // 2
    core = lax.rem(mine, 2)
    others = []
    for step in range(1, chips):
        for flip in range(2):
            others.append(lax.rem(chip + step, chips) * 2 + lax.rem(core + flip, 2))
    return others + [chip * 2 + 1 - core]


def kernel(
    n_tm, n_chan,
    vis_hbm, gain_hbm, pairs_hbm, bands_hbm, map_hbm, order_hbm, avg_ref, early_tiles, late_tiles,
    vis_ref, gain_ref, pairs_ref, bands_ref, map_ref, order_ref, local, index,
    send, turned, gain_send, gains, table, chosen, partials, calibrated, early_send, late_send,
    turn_out, turn_in, gain_out, gain_in, tile_out, tile_in,
):
    me = lax.axis_index("tm")
    mine = lax.axis_index("chan")
    baselines = vis_ref.shape[1]
    width = vis_ref.shape[2]
    rows = baselines // n_tm
    stations = gain_ref.shape[1]
    padded = gain_send.shape[2]
    tile_rows = early_tiles.shape[1] // 2
    n_tiles = tile_rows * n_tm
    times = map_ref.shape[0]
    first_at, second_at, time_at, chan_at = range(times, times + 4)
    around = [step + lax.div(step - me + n_tm, n_tm) for step in range(n_tm - 1)]
    across = peers(mine, n_chan)

    sources = (
        gain_hbm.at[0:4], order_hbm, gain_hbm.at[4:8], vis_hbm.at[0], pairs_hbm, bands_hbm, map_hbm
    )
    targets = (
        gain_ref.at[0:4], order_ref, gain_ref.at[4:8], vis_ref, pairs_ref, bands_ref, map_ref
    )
    loads = [
        pltpu.make_async_copy(source, target, local.at[i])
        for i, (source, target) in enumerate(zip(sources, targets))
    ]
    for load in loads:
        load.start()

    barrier = pltpu.get_barrier_semaphore()
    for other in around:
        pl.semaphore_signal(barrier, inc=1, device_id={"tm": other}, device_id_type=MESH)
    for other in across:
        pl.semaphore_signal(barrier, inc=1, device_id={"chan": other}, device_id_type=MESH)

    def pack_gains(half):
        for c in range(n_chan):
            block = jnp.concatenate(
                [
                    gain_ref[4 * half + i, :, c * width : (c + 1) * width] for i in range(4)
                ],
                axis=1,
            )
            if padded > stations:
                block = jnp.concatenate(
                    [block, jnp.zeros((padded - stations, 4 * width), F32)], axis=0
                )
            gain_send[half, c] = block.astype(BF16)

    def gain_copy(half, other, slot):
        return pltpu.make_async_remote_copy(
            src_ref=gain_send.at[half, other],
            dst_ref=gains.at[half, slot],
            send_sem=gain_out.at[half, other],
            recv_sem=gain_in.at[half, slot],
            device_id={"chan": other},
            device_id_type=MESH,
        )

    def turn_copy(other, slot):
        return pltpu.make_async_remote_copy(
            src_ref=send.at[other],
            dst_ref=turned.at[slot],
            send_sem=turn_out.at[other],
            recv_sem=turn_in.at[slot],
            device_id={"tm": other},
            device_id_type=MESH,
        )

    def tile_copy(chunk, other, slot):
        source, target = ((early_send, early_tiles), (late_send, late_tiles))[chunk]
        return pltpu.make_async_remote_copy(
            src_ref=source.at[other],
            dst_ref=target.at[slot],
            send_sem=tile_out.at[chunk, other],
            recv_sem=tile_in.at[chunk, slot],
            device_id={"tm": other},
            device_id_type=MESH,
        )

    copies = []

    def start(copy):
        copy.start()
        copies.append(copy)

    loads[0].wait()
    pack_gains(0)
    loads[1].wait()
    place = jnp.where(order_ref[...] == iota((baselines, baselines), 0), 1.0, 0.0)
    place = place.T.astype(BF16)

    pl.semaphore_wait(barrier, n_tm + n_chan - 2)

    for other in across:
        start(gain_copy(0, other, mine))
    loads[2].wait()
    pack_gains(1)
    for other in across:
        start(gain_copy(1, other, mine))

    loads[3].wait()
    raw = jnp.concatenate([vis_ref[i] for i in range(8)], axis=1)
    send[...] = dot(place, raw).astype(BF16).reshape(send.shape)
    for other in around:
        start(turn_copy(other, me))

    turned[me] = send[me]
    gains[0, mine] = gain_send[0, mine]
    gains[1, mine] = gain_send[1, mine]
    means = channel_means(width)
    stacked = jnp.concatenate(
        [means[:, k * width : (k + 1) * width] for k in range(CLOG)], axis=0
    )
    for load in loads[4:]:
        load.wait()
    index[...] = jnp.zeros_like(index)
    index[:times] = map_ref[...].astype(F32)
    index[first_at : second_at + 1] = pairs_ref[...].astype(F32)
    index[time_at : chan_at + 1] = bands_ref[...].astype(F32)
    table[...] = lax.dot_general(
        place, index[...].astype(BF16), (((1,), (1,)), ((), ())), preferred_element_type=F32
    )

    ids = iota((1, n_chan * padded), 1)
    if padded > stations:
        lane = ids
        for c in range(n_chan):
            inside = (lane >= c * padded) & (lane < c * padded + stations)
            ids = jnp.where(inside, lane - c * (padded - stations), ids)
            ids = jnp.where((lane >= c * padded + stations) & (lane < (c + 1) * padded), -1, ids)
    here = pl.ds(pl.multiple_of(me * rows, rows), rows)
    at_all = table[...].astype(jnp.int32)
    at_here = table[here, :].astype(jnp.int32)
    pick = jnp.concatenate(
        [
            one_hot(at_all[:, first_at : first_at + 1], ids),
            one_hot(at_all[:, second_at : second_at + 1], ids),
            one_hot(at_here[:, first_at : first_at + 1], ids),
            one_hot(at_here[:, second_at : second_at + 1], ids),
        ],
        axis=0,
    )
    period = jnp.left_shift(jnp.ones((baselines, 1), jnp.int32), at_all[:, time_at : time_at + 1])
    begin = me - (me & (period - 1))
    lane = iota((baselines, LANES), 1)
    tile = jnp.sum(
        jnp.where(lane == begin, table[...], 0.0), axis=1, keepdims=True
    ).astype(jnp.int32)
    tile = tile + n_tiles * at_all[:, chan_at : chan_at + 1]
    n_share = (CLOG + 1) * n_tiles
    wide = -(-n_share // LANES) * LANES
    share = jnp.where(tile == iota((baselines, wide), 1), 1.0 / period.astype(F32), 0.0)
    share = share.T[:n_share].astype(BF16)

    def block_rows(k):
        at = pl.ds(pl.multiple_of(k * rows, rows), rows)
        return at, pl.ds(pl.multiple_of(baselines + k * rows, rows), rows)

    for other in across:
        gain_copy(0, other, other).wait_recv()
    chosen[0] = dot(pick, gains[0].reshape(n_chan * padded, 4 * width))

    def calibrate_early(k, carry):
        at, at_second = block_rows(k)
        coherency = as_matrix(split(send[k].astype(F32), width))
        partial = row_times(as_row(split(chosen[0, at, :], width)), coherency)
        partials[at, :] = flat(partial)
        entry = times_row_conj(partial, as_row(split(chosen[0, at_second, :], width)))
        calibrated[at, : 2 * width] = flat([entry]).astype(BF16)
        return carry

    lax.fori_loop(0, n_tm, calibrate_early, 0, unroll=4)
    early_send[...] = tile_sums(share, calibrated[:, : 2 * width], stacked, n_tm, width)
    for other in around:
        start(tile_copy(0, other, me))
    early_tiles[me] = early_send[me]

    for other in across:
        gain_copy(1, other, other).wait_recv()
    chosen[1] = dot(pick, gains[1].reshape(n_chan * padded, 4 * width))

    def calibrate_late(k, carry):
        at, at_second = block_rows(k)
        coherency = as_matrix(split(send[k].astype(F32), width))
        upper = as_row(split(partials[at, :], width))
        lower = row_times(as_row(split(chosen[1, at, :], width)), coherency)
        right_upper = as_row(split(chosen[0, at_second, :], width))
        right_lower = as_row(split(chosen[1, at_second, :], width))
        entries = [
            times_row_conj(upper, right_lower),
            times_row_conj(lower, right_upper),
            times_row_conj(lower, right_lower),
        ]
        calibrated[at, 2 * width :] = flat(entries).astype(BF16)
        return carry

    lax.fori_loop(0, n_tm, calibrate_late, 0, unroll=4)
    late_send[...] = tile_sums(share, calibrated[:, 2 * width :], stacked, n_tm, width)
    for other in around:
        start(tile_copy(1, other, me))
    late_tiles[me] = late_send[me]

    for other in around:
        turn_copy(other, other).wait_recv()
    ends = (2 * baselines, 2 * baselines + rows, 2 * baselines + 2 * rows)
    left, right = [
        split(chosen[0, ends[j] : ends[j + 1], :], width)
        + split(chosen[1, ends[j] : ends[j + 1], :], width)
        for j in range(2)
    ]

    def calibrate_time(t, carry):
        result = jones_apply(left, split(turned[t].astype(F32), width), right)
        at = pl.ds(pl.multiple_of(t * rows, rows), rows)
        calibrated[at, :] = jnp.concatenate(result, axis=1).astype(BF16)
        return carry

    lax.fori_loop(0, n_tm, calibrate_time, 0, unroll=4)
    group = 2**TLOG
    time_level = jnp.broadcast_to(at_here[:, time_at : time_at + 1], (rows, width))
    chan_level = jnp.broadcast_to(at_here[:, chan_at : chan_at + 1], (rows, width))
    chan_level = jnp.concatenate([chan_level] * group, axis=0)
    for first in range(0, n_tm, group):
        at = slice(first * rows, (first + group) * rows)
        for i in range(8):
            part = channel_average(
                calibrated[at, i * width : (i + 1) * width], means, chan_level, width
            )
            current = [part[t * rows : (t + 1) * rows] for t in range(group)]
            result = list(current)
            for k in range(1, TLOG + 1):
                current = [
                    0.5 * (current[2 * j] + current[2 * j + 1]) for j in range(len(current) // 2)
                ]
                result = [
                    jnp.where(time_level >= k, current[t >> k], result[t]) for t in range(group)
                ]
            for t in range(group):
                avg_ref[first + t, i] = result[t].astype(BF16)

    for chunk in range(2):
        for other in around:
            tile_copy(chunk, other, other).wait_recv()
    for copy in copies:
        copy.wait_send()


def write_kernel(avg_ref, early_ref, late_ref, avg_hbm, grid_hbm, grid, done):
    averaged = pltpu.make_async_copy(avg_ref, avg_hbm, done.at[0])
    averaged.start()
    tile_rows = grid.shape[0]
    first = 0
    for ref in (early_ref, late_ref):
        total = ref[0].astype(F32)
        for m in range(1, ref.shape[0]):
            total = total + ref[m].astype(F32)
        count = ref.shape[1] // tile_rows
        for i in range(count):
            grid[:, first + i, :] = total[i * tile_rows : (i + 1) * tile_rows]
        first += count
    gridded = pltpu.make_async_copy(grid, grid_hbm, done.at[1])
    gridded.start()
    averaged.wait()
    gridded.wait()


def shards(n_tm, n_chan, tile_count, visibilities, station_gains, station_pairs, average_bands, tile_map, baseline_order):
    baselines, width = visibilities.shape[2:]
    rows = baselines // n_tm
    stations = station_gains.shape[1]
    padded = -(-stations // 16) * 16
    tile_rows = tile_count // n_tm
    vmem = pl.BlockSpec(memory_space=pltpu.VMEM)
    dma = pltpu.SemaphoreType.DMA
    hbm = functools.partial(pltpu.with_memory_space_constraint, memory_space=pltpu.HBM)
    near = functools.partial(pltpu.with_memory_space_constraint, memory_space=pltpu.VMEM)
    averaged, early, late = pl.pallas_call(
        functools.partial(kernel, n_tm, n_chan),
        out_shape=(
            pltpu.VMEM((n_tm, 8, rows, width), BF16),
            pltpu.VMEM((n_tm, 2 * tile_rows, width), BF16),
            pltpu.VMEM((n_tm, 6 * tile_rows, width), BF16),
        ),
        in_specs=[pl.BlockSpec(memory_space=pl.ANY)] * 6,
        out_specs=(vmem,) * 3,
        scratch_shapes=[
            pltpu.VMEM((8, baselines, width), BF16),
            pltpu.VMEM(station_gains.shape, F32),
            pltpu.VMEM((2, baselines), jnp.int32),
            pltpu.VMEM((2, baselines), jnp.int32),
            pltpu.VMEM((n_tm, baselines), jnp.int32),
            pltpu.VMEM((1, baselines), jnp.int32),
            dma((7,)),
            pltpu.VMEM((LANES, baselines), F32),
            pltpu.VMEM((n_tm, rows, 8 * width), BF16),
            pltpu.VMEM((n_tm, rows, 8 * width), BF16),
            pltpu.VMEM((2, n_chan, padded, 4 * width), BF16),
            pltpu.VMEM((2, n_chan, padded, 4 * width), BF16),
            pltpu.VMEM((baselines, LANES), F32),
            pltpu.VMEM((2, 2 * baselines + 2 * rows, 4 * width), F32),
            pltpu.VMEM((baselines, 4 * width), F32),
            pltpu.VMEM((baselines, 8 * width), BF16),
            pltpu.VMEM((n_tm, 2 * tile_rows, width), BF16),
            pltpu.VMEM((n_tm, 6 * tile_rows, width), BF16),
            dma((n_tm,)),
            dma((n_tm,)),
            dma((2, n_chan)),
            dma((2, n_chan)),
            dma((2, n_tm)),
            dma((2, n_tm)),
        ],
        compiler_params=pltpu.CompilerParams(
            collective_id=0, has_side_effects=True, vmem_limit_bytes=40 * 2**20
        ),
        cost_estimate=pl.CostEstimate(
            flops=2 * 10**8, bytes_accessed=2 * 10**6, transcendentals=0
        ),
    )(
        hbm(visibilities),
        hbm(station_gains),
        hbm(station_pairs.T),
        hbm(average_bands.T),
        hbm(tile_map.T),
        hbm(baseline_order.reshape(1, baselines)),
    )
    return pl.pallas_call(
        write_kernel,
        out_shape=(
            pltpu.HBM(averaged.shape, BF16),
            pltpu.HBM((tile_rows, 8, width), F32),
        ),
        in_specs=[vmem] * 3,
        out_specs=(pl.BlockSpec(memory_space=pltpu.HBM),) * 2,
        scratch_shapes=[pltpu.VMEM((tile_rows, 8, width), F32), dma((2,))],
        compiler_params=pltpu.CompilerParams(vmem_limit_bytes=8 * 2**20),
        cost_estimate=pl.CostEstimate(flops=10**6, bytes_accessed=10**6, transcendentals=0),
    )(near(averaged), near(early), near(late))


def solution(mesh):
    n_tm, n_chan = mesh.shape["tm"], mesh.shape["chan"]
    tile_count = 8 * n_tm
    return jax.shard_map(
        functools.partial(shards, n_tm, n_chan, tile_count),
        mesh=mesh,
        in_specs=(P("tm", None, None, "chan"), P(None, "chan", None), P(), P(), P(), P()),
        out_specs=(P(None, None, "tm", "chan"), P("tm", None, "chan")),
        check_vma=False,
    )
```

```python
import functools

import jax
import jax.numpy as jnp
from jax import lax
from jax.experimental import pallas as pl
from jax.experimental.pallas import tpu as pltpu
from jax.sharding import PartitionSpec as P

TLOG = 3
CLOG = 2
LANES = 128
MESH = pl.DeviceIdType.MESH
F32 = jnp.float32
BF16 = jnp.bfloat16


def product(left, right):
    return (left[0] * right[0] - left[1] * right[1], left[0] * right[1] + left[1] * right[0])


def product_conj(left, right):
    return (left[0] * right[0] + left[1] * right[1], left[1] * right[0] - left[0] * right[1])


def add_pair(left, right):
    return (left[0] + right[0], left[1] + right[1])


def as_matrix(components):
    return [
        [(components[0], components[1]), (components[2], components[3])],
        [(components[4], components[5]), (components[6], components[7])],
    ]


def jones_apply(first, middle, second):
    left_gain = as_matrix(first)
    coherency = as_matrix(middle)
    right_gain = as_matrix(second)
    partial_rows = [
        [
            add_pair(
                product(left_gain[i][0], coherency[0][k]), product(left_gain[i][1], coherency[1][k])
            )
            for k in range(2)
        ]
        for i in range(2)
    ]
    result = []
    for i in range(2):
        for c in range(2):
            element = add_pair(
                product_conj(partial_rows[i][0], right_gain[c][0]),
                product_conj(partial_rows[i][1], right_gain[c][1]),
            )
            result.extend(element)
    return result


def split(values, width):
    return [values[:, i * width : (i + 1) * width] for i in range(values.shape[1] // width)]


def iota(shape, axis):
    return lax.broadcasted_iota(jnp.int32, shape, axis)


def dot(left, right):
    return jnp.dot(left, right, preferred_element_type=F32)


def one_hot(column, ids):
    return jnp.where(column == ids, 1.0, 0.0).astype(BF16)


def channel_means(width):
    row = iota((width, width), 0)
    column = iota((width, width), 1)
    means = []
    for level in range(1, CLOG + 1):
        same = (row >> level) == (column >> level)
        means.append(jnp.where(same, 2.0**-level, 0.0))
    return jnp.concatenate(means, axis=1).astype(BF16)


def row_times(row, middle):
    return [
        add_pair(product(row[0], middle[0][b]), product(row[1], middle[1][b])) for b in range(2)
    ]


def times_row_conj(partial, row):
    return add_pair(product_conj(partial[0], row[0]), product_conj(partial[1], row[1]))


def as_row(components):
    return [(components[0], components[1]), (components[2], components[3])]


def flat(pairs):
    return jnp.concatenate([part for pair in pairs for part in pair], axis=1)


def tile_sums(share, samples, means, blocks, width):
    count = samples.shape[1] // width
    summed = dot(share, samples)
    n_tiles = share.shape[0] // (CLOG + 1)
    levels = []
    for i in range(count):
        part = summed[:, i * width : (i + 1) * width]
        levels.append(
            jnp.concatenate(
                [part[k * n_tiles : (k + 1) * n_tiles] for k in range(1, CLOG + 1)], axis=1
            )
        )
    spread = dot(jnp.concatenate(levels, axis=0).astype(BF16), means)
    result = []
    for i in range(count):
        part = summed[:n_tiles, i * width : (i + 1) * width]
        part = part + spread[i * n_tiles : (i + 1) * n_tiles]
        result.append(part.reshape(blocks, n_tiles // blocks, width))
    return jnp.concatenate(result, axis=1).astype(BF16)


def channel_average(samples, means, level, width):
    averaged = dot(samples, means)
    result = samples.astype(F32)
    for k in range(1, CLOG + 1):
        result = jnp.where(level >= k, averaged[:, (k - 1) * width : k * width], result)
    return result


def peers(mine, count):
    chips = count // 2
    chip = mine // 2
    core = lax.rem(mine, 2)
    others = []
    for step in range(1, chips):
        for flip in range(2):
            others.append(lax.rem(chip + step, chips) * 2 + lax.rem(core + flip, 2))
    return others + [chip * 2 + 1 - core]


def kernel(
    n_tm, n_chan,
    vis_hbm, gain_hbm, pairs_hbm, bands_hbm, map_hbm, order_hbm, avg_ref, early_tiles, late_tiles,
    vis_ref, gain_ref, pairs_ref, bands_ref, map_ref, order_ref, local, index,
    send, turned, gain_send, gains, table, chosen, partials, calibrated, early_send, late_send,
    turn_out, turn_in, gain_out, gain_in, tile_out, tile_in,
):
    me = lax.axis_index("tm")
    mine = lax.axis_index("chan")
    baselines = vis_ref.shape[1]
    width = vis_ref.shape[2]
    rows = baselines // n_tm
    stations = gain_ref.shape[1]
    padded = gain_send.shape[2]
    tile_rows = early_tiles.shape[1] // 2
    n_tiles = tile_rows * n_tm
    times = map_ref.shape[0]
    first_at, second_at, time_at, chan_at = range(times, times + 4)
    around = [step + lax.div(step - me + n_tm, n_tm) for step in range(n_tm - 1)]
    across = peers(mine, n_chan)

    sources = (
        gain_hbm.at[0:4], order_hbm, gain_hbm.at[4:8], vis_hbm.at[0], pairs_hbm, bands_hbm, map_hbm
    )
    targets = (
        gain_ref.at[0:4], order_ref, gain_ref.at[4:8], vis_ref, pairs_ref, bands_ref, map_ref
    )
    loads = [
        pltpu.make_async_copy(source, target, local.at[i])
        for i, (source, target) in enumerate(zip(sources, targets))
    ]
    for load in loads:
        load.start()

    barrier = pltpu.get_barrier_semaphore()
    for other in around:
        pl.semaphore_signal(barrier, inc=1, device_id={"tm": other}, device_id_type=MESH)
    for other in across:
        pl.semaphore_signal(barrier, inc=1, device_id={"chan": other}, device_id_type=MESH)

    def pack_gains(half):
        for c in range(n_chan):
            block = jnp.concatenate(
                [
                    gain_ref[4 * half + i, :, c * width : (c + 1) * width] for i in range(4)
                ],
                axis=1,
            )
            if padded > stations:
                block = jnp.concatenate(
                    [block, jnp.zeros((padded - stations, 4 * width), F32)], axis=0
                )
            gain_send[half, c] = block.astype(BF16)

    def gain_copy(half, other, slot):
        return pltpu.make_async_remote_copy(
            src_ref=gain_send.at[half, other],
            dst_ref=gains.at[half, slot],
            send_sem=gain_out.at[half, other],
            recv_sem=gain_in.at[half, slot],
            device_id={"chan": other},
            device_id_type=MESH,
        )

    def turn_copy(other, slot):
        return pltpu.make_async_remote_copy(
            src_ref=send.at[other],
            dst_ref=turned.at[slot],
            send_sem=turn_out.at[other],
            recv_sem=turn_in.at[slot],
            device_id={"tm": other},
            device_id_type=MESH,
        )

    def tile_copy(chunk, other, slot):
        source, target = ((early_send, early_tiles), (late_send, late_tiles))[chunk]
        return pltpu.make_async_remote_copy(
            src_ref=source.at[other],
            dst_ref=target.at[slot],
            send_sem=tile_out.at[chunk, other],
            recv_sem=tile_in.at[chunk, slot],
            device_id={"tm": other},
            device_id_type=MESH,
        )

    copies = []

    def start(copy):
        copy.start()
        copies.append(copy)

    loads[0].wait()
    pack_gains(0)
    loads[1].wait()
    place = jnp.where(order_ref[...] == iota((baselines, baselines), 0), 1.0, 0.0)
    place = place.T.astype(BF16)

    means = channel_means(width)
    stacked = jnp.concatenate(
        [means[:, k * width : (k + 1) * width] for k in range(CLOG)], axis=0
    )
    for load in loads[4:]:
        load.wait()
    index[...] = jnp.zeros_like(index)
    index[:times] = map_ref[...].astype(F32)
    index[first_at : second_at + 1] = pairs_ref[...].astype(F32)
    index[time_at : chan_at + 1] = bands_ref[...].astype(F32)
    table[...] = lax.dot_general(
        place, index[...].astype(BF16), (((1,), (1,)), ((), ())), preferred_element_type=F32
    )

    ids = iota((1, n_chan * padded), 1)
    if padded > stations:
        lane = ids
        for c in range(n_chan):
            inside = (lane >= c * padded) & (lane < c * padded + stations)
            ids = jnp.where(inside, lane - c * (padded - stations), ids)
            ids = jnp.where((lane >= c * padded + stations) & (lane < (c + 1) * padded), -1, ids)
    here = pl.ds(pl.multiple_of(me * rows, rows), rows)
    at_all = table[...].astype(jnp.int32)
    at_here = table[here, :].astype(jnp.int32)
    pick = jnp.concatenate(
        [
            one_hot(at_all[:, first_at : first_at + 1], ids),
            one_hot(at_all[:, second_at : second_at + 1], ids),
            one_hot(at_here[:, first_at : first_at + 1], ids),
            one_hot(at_here[:, second_at : second_at + 1], ids),
        ],
        axis=0,
    )
    period = jnp.left_shift(jnp.ones((baselines, 1), jnp.int32), at_all[:, time_at : time_at + 1])
    begin = me - (me & (period - 1))
    lane = iota((baselines, LANES), 1)
    tile = jnp.sum(
        jnp.where(lane == begin, table[...], 0.0), axis=1, keepdims=True
    ).astype(jnp.int32)
    tile = tile + n_tiles * at_all[:, chan_at : chan_at + 1]
    n_share = (CLOG + 1) * n_tiles
    wide = -(-n_share // LANES) * LANES
    share = jnp.where(tile == iota((baselines, wide), 1), 1.0 / period.astype(F32), 0.0)
    share = share.T[:n_share].astype(BF16)

    pl.semaphore_wait(barrier, n_tm + n_chan - 2)

    for other in across:
        start(gain_copy(0, other, mine))
    loads[2].wait()
    pack_gains(1)
    for other in across:
        start(gain_copy(1, other, mine))

    loads[3].wait()
    raw = jnp.concatenate([vis_ref[i] for i in range(8)], axis=1)
    send[...] = dot(place, raw).astype(BF16).reshape(send.shape)
    for other in around:
        start(turn_copy(other, me))

    turned[me] = send[me]
    gains[0, mine] = gain_send[0, mine]
    gains[1, mine] = gain_send[1, mine]
    def block_rows(k):
        at = pl.ds(pl.multiple_of(k * rows, rows), rows)
        return at, pl.ds(pl.multiple_of(baselines + k * rows, rows), rows)

    for other in across:
        gain_copy(0, other, other).wait_recv()
    chosen[0] = dot(pick, gains[0].reshape(n_chan * padded, 4 * width))

    def calibrate_early(k, carry):
        at, at_second = block_rows(k)
        coherency = as_matrix(split(send[k].astype(F32), width))
        partial = row_times(as_row(split(chosen[0, at, :], width)), coherency)
        partials[at, :] = flat(partial)
        entry = times_row_conj(partial, as_row(split(chosen[0, at_second, :], width)))
        calibrated[at, : 2 * width] = flat([entry]).astype(BF16)
        return carry

    lax.fori_loop(0, n_tm, calibrate_early, 0, unroll=2)
    early_send[...] = tile_sums(share, calibrated[:, : 2 * width], stacked, n_tm, width)
    for other in around:
        start(tile_copy(0, other, me))
    early_tiles[me] = early_send[me]

    for other in across:
        gain_copy(1, other, other).wait_recv()
    chosen[1] = dot(pick, gains[1].reshape(n_chan * padded, 4 * width))

    def calibrate_late(k, carry):
        at, at_second = block_rows(k)
        coherency = as_matrix(split(send[k].astype(F32), width))
        upper = as_row(split(partials[at, :], width))
        lower = row_times(as_row(split(chosen[1, at, :], width)), coherency)
        right_upper = as_row(split(chosen[0, at_second, :], width))
        right_lower = as_row(split(chosen[1, at_second, :], width))
        entries = [
            times_row_conj(upper, right_lower),
            times_row_conj(lower, right_upper),
            times_row_conj(lower, right_lower),
        ]
        calibrated[at, 2 * width :] = flat(entries).astype(BF16)
        return carry

    lax.fori_loop(0, n_tm, calibrate_late, 0, unroll=2)
    late_send[...] = tile_sums(share, calibrated[:, 2 * width :], stacked, n_tm, width)
    for other in around:
        start(tile_copy(1, other, me))
    late_tiles[me] = late_send[me]

    for other in around:
        turn_copy(other, other).wait_recv()
    ends = (2 * baselines, 2 * baselines + rows, 2 * baselines + 2 * rows)
    left, right = [
        split(chosen[0, ends[j] : ends[j + 1], :], width)
        + split(chosen[1, ends[j] : ends[j + 1], :], width)
        for j in range(2)
    ]

    def calibrate_time(t, carry):
        result = jones_apply(left, split(turned[t].astype(F32), width), right)
        at = pl.ds(pl.multiple_of(t * rows, rows), rows)
        calibrated[at, :] = jnp.concatenate(result, axis=1).astype(BF16)
        return carry

    lax.fori_loop(0, n_tm, calibrate_time, 0, unroll=2)
    group = 2**TLOG
    time_level = jnp.broadcast_to(at_here[:, time_at : time_at + 1], (rows, width))
    chan_level = jnp.broadcast_to(at_here[:, chan_at : chan_at + 1], (rows, width))
    chan_level = jnp.concatenate([chan_level] * group, axis=0)
    for first in range(0, n_tm, group):
        at = slice(first * rows, (first + group) * rows)
        for i in range(8):
            part = channel_average(
                calibrated[at, i * width : (i + 1) * width], means, chan_level, width
            )
            current = [part[t * rows : (t + 1) * rows] for t in range(group)]
            result = list(current)
            for k in range(1, TLOG + 1):
                current = [
                    0.5 * (current[2 * j] + current[2 * j + 1]) for j in range(len(current) // 2)
                ]
                result = [
                    jnp.where(time_level >= k, current[t >> k], result[t]) for t in range(group)
                ]
            for t in range(group):
                avg_ref[first + t, i] = result[t].astype(BF16)

    for chunk in range(2):
        for other in around:
            tile_copy(chunk, other, other).wait_recv()
    for copy in copies:
        copy.wait_send()


def write_kernel(avg_ref, early_ref, late_ref, avg_hbm, grid_hbm, grid, done):
    averaged = pltpu.make_async_copy(avg_ref, avg_hbm, done.at[0])
    averaged.start()
    tile_rows = grid.shape[0]
    first = 0
    for ref in (early_ref, late_ref):
        total = ref[0].astype(F32)
        for m in range(1, ref.shape[0]):
            total = total + ref[m].astype(F32)
        count = ref.shape[1] // tile_rows
        for i in range(count):
            grid[:, first + i, :] = total[i * tile_rows : (i + 1) * tile_rows]
        first += count
    gridded = pltpu.make_async_copy(grid, grid_hbm, done.at[1])
    gridded.start()
    averaged.wait()
    gridded.wait()


def shards(n_tm, n_chan, tile_count, visibilities, station_gains, station_pairs, average_bands, tile_map, baseline_order):
    baselines, width = visibilities.shape[2:]
    rows = baselines // n_tm
    stations = station_gains.shape[1]
    padded = -(-stations // 16) * 16
    tile_rows = tile_count // n_tm
    vmem = pl.BlockSpec(memory_space=pltpu.VMEM)
    dma = pltpu.SemaphoreType.DMA
    hbm = functools.partial(pltpu.with_memory_space_constraint, memory_space=pltpu.HBM)
    near = functools.partial(pltpu.with_memory_space_constraint, memory_space=pltpu.VMEM)
    averaged, early, late = pl.pallas_call(
        functools.partial(kernel, n_tm, n_chan),
        out_shape=(
            pltpu.VMEM((n_tm, 8, rows, width), BF16),
            pltpu.VMEM((n_tm, 2 * tile_rows, width), BF16),
            pltpu.VMEM((n_tm, 6 * tile_rows, width), BF16),
        ),
        in_specs=[pl.BlockSpec(memory_space=pl.ANY)] * 6,
        out_specs=(vmem,) * 3,
        scratch_shapes=[
            pltpu.VMEM((8, baselines, width), BF16),
            pltpu.VMEM(station_gains.shape, F32),
            pltpu.VMEM((2, baselines), jnp.int32),
            pltpu.VMEM((2, baselines), jnp.int32),
            pltpu.VMEM((n_tm, baselines), jnp.int32),
            pltpu.VMEM((1, baselines), jnp.int32),
            dma((7,)),
            pltpu.VMEM((LANES, baselines), F32),
            pltpu.VMEM((n_tm, rows, 8 * width), BF16),
            pltpu.VMEM((n_tm, rows, 8 * width), BF16),
            pltpu.VMEM((2, n_chan, padded, 4 * width), BF16),
            pltpu.VMEM((2, n_chan, padded, 4 * width), BF16),
            pltpu.VMEM((baselines, LANES), F32),
            pltpu.VMEM((2, 2 * baselines + 2 * rows, 4 * width), F32),
            pltpu.VMEM((baselines, 4 * width), F32),
            pltpu.VMEM((baselines, 8 * width), BF16),
            pltpu.VMEM((n_tm, 2 * tile_rows, width), BF16),
            pltpu.VMEM((n_tm, 6 * tile_rows, width), BF16),
            dma((n_tm,)),
            dma((n_tm,)),
            dma((2, n_chan)),
            dma((2, n_chan)),
            dma((2, n_tm)),
            dma((2, n_tm)),
        ],
        compiler_params=pltpu.CompilerParams(
            collective_id=0, has_side_effects=True, vmem_limit_bytes=40 * 2**20
        ),
        cost_estimate=pl.CostEstimate(
            flops=2 * 10**8, bytes_accessed=2 * 10**6, transcendentals=0
        ),
    )(
        hbm(visibilities),
        hbm(station_gains),
        hbm(station_pairs.T),
        hbm(average_bands.T),
        hbm(tile_map.T),
        hbm(baseline_order.reshape(1, baselines)),
    )
    return pl.pallas_call(
        write_kernel,
        out_shape=(
            pltpu.HBM(averaged.shape, BF16),
            pltpu.HBM((tile_rows, 8, width), F32),
        ),
        in_specs=[vmem] * 3,
        out_specs=(pl.BlockSpec(memory_space=pltpu.HBM),) * 2,
        scratch_shapes=[pltpu.VMEM((tile_rows, 8, width), F32), dma((2,))],
        compiler_params=pltpu.CompilerParams(vmem_limit_bytes=8 * 2**20),
        cost_estimate=pl.CostEstimate(flops=10**6, bytes_accessed=10**6, transcendentals=0),
    )(near(averaged), near(early), near(late))


def solution(mesh):
    n_tm, n_chan = mesh.shape["tm"], mesh.shape["chan"]
    tile_count = 8 * n_tm
    return jax.shard_map(
        functools.partial(shards, n_tm, n_chan, tile_count),
        mesh=mesh,
        in_specs=(P("tm", None, None, "chan"), P(None, "chan", None), P(), P(), P(), P()),
        out_specs=(P(None, None, "tm", "chan"), P("tm", None, "chan")),
        check_vma=False,
    )
```
